32 devices in a mesh: tm: 8 (over z, y), orb: 4 (over x, core).
Axes of the slice: x: 2, y: 2, z: 4, core: 2. Of those that a mesh axis runs over, the one named last changes fastest.
Arguments:
- self_energy: float32 [8, 2, 8, 1024, 2048], P('tm', None, None, 'orb'), may hold values from -0.0625 to 0.0625
- history: float32 [8, 2, 1024, 1024], P('tm', None, 'orb'), may hold values from -8 to 8
- memory: int32 [1], replicated, may hold values from 3 to 8
- startup_cut: int32 [8], P('tm'), may hold values from 0 to 2048
- weight_index: int32 [8, 8], P('tm'), may hold values from 0 to 15
- weight_table: float32 [16], replicated, may hold values from 0.3 to 3
Outputs:
- collision: float32 [8, 2048, 1024], P('tm', 'orb')
The draws below stay inside these ranges and needn't reach their ends.
All inputs are finite; a program needn't handle non-finite values.
Results may differ from the reference program's by a relative error of at most 0.0003.
Values sent between devices are 32-bit elements; how exact they have to be, the bound alone decides.
No kernel may reach another device: no remote copies, remote signals or barrier semaphores. Data moves between devices by JAX's collectives and lax.ppermute only.
A program may use at most 128 MiB of HBM per device.

```python
import math
import jax
import jax.numpy as jnp
from jax import lax

NORB = 1024
LAGS = 8
R = 2048
NQ = 16
NBLK = 8


def place_ends(drawn, own_key, low, largest):
    spot = [jax.random.randint(jax.random.fold_in(own_key, axis), (), 0, length) for axis, length in enumerate(drawn.shape)]
    main_axis = drawn.shape.index(max(drawn.shape))
    beside = spot[:main_axis] + [(spot[main_axis] + 1) % drawn.shape[main_axis]] + spot[main_axis + 1:]
    return drawn.at[tuple(spot)].set(low).at[tuple(beside)].set(largest)


def strengthened(drawn, own_key, source, target, blocks, factor):
    owner, partner = [(jnp.arange(drawn.shape[dim]) // (drawn.shape[dim] // blocks)).reshape([-1 if axis == dim else 1 for axis in range(drawn.ndim)]) for dim in (source, target)]
    chosen = jax.random.permutation(own_key, blocks)[partner]
    strong = (owner == chosen) | (owner == (partner + blocks // 2) % blocks)
    return jnp.where(strong, factor * drawn, drawn)


def level_of(own_key, dims, split, smallest, high):
    factor_of = 1.0
    for axis_at, parts in split:
        heights = jax.random.uniform(jax.random.fold_in(jax.random.fold_in(own_key, 6), axis_at), (parts,), jnp.float32, smallest / len(split), high / len(split))
        factor_of = factor_of * jnp.repeat(jnp.exp(heights), dims[axis_at] // parts).reshape((-1,) + (1,) * (len(dims) - 1 - axis_at))
    return factor_of


def noise(key, extent, deviation, bound, cuts=(), held_as=jnp.bfloat16):
    entries = deviation * jax.random.normal(key, extent, jnp.float32)
    if cuts:
        entries = entries * level_of(key, extent, cuts, -0.22, 0.18)
    return jnp.clip(entries, -bound, bound).astype(held_as)


def gaussian_with(key, dims, deviation, most, shards, heavy, kind=jnp.bfloat16):
    result = deviation * jax.random.normal(key, dims, jnp.float32)
    if shards:
        result = result * level_of(key, dims, shards, -0.22, 0.18)
    return jnp.clip(strengthened(result, jax.random.fold_in(key, 3), *heavy), -most, most).astype(kind)


def setup_inputs(seed: int = 0) -> dict:
    key_list = jax.random.split(jax.random.key(seed), 7)
    return {
        "self_energy": gaussian_with(key_list[0], (NBLK, 2, LAGS, NORB, R), (2 * NORB * LAGS) ** -0.5, 0.0625, ((0, 8), (3, 4)), (3, 4, 4, 2.0), jnp.float32),
        "history": noise(key_list[1], (NBLK, 2, NORB, NORB), 1.0, 8.0, ((0, 8), (2, 4)), jnp.float32),
        "memory": jax.random.randint(key_list[2], (1,), 3, LAGS + 1).astype(jnp.int32),
        "startup_cut": place_ends(jax.random.randint(key_list[3], (NBLK,), 0, R + 1), jax.random.fold_in(key_list[3], 1), 0, R).astype(jnp.int32),
        "weight_index": place_ends(jax.random.randint(key_list[4], (NBLK, LAGS), 0, NQ), jax.random.fold_in(key_list[4], 1), 0, NQ - 1).astype(jnp.int32),
        "weight_table": jnp.clip(jnp.exp(jax.random.uniform(key_list[5], (NQ,), jnp.float32, math.log(0.3), math.log(3.0))), 0.3, 3.0),
    }


def reference(self_energy, history, memory, startup_cut, weight_index, weight_table):
    padded = jnp.concatenate([jnp.zeros((LAGS - 1, 2, NORB, NORB), jnp.float32), history], axis=0)
    lag_ids = jnp.arange(LAGS, dtype=jnp.int32)[:, None]
    row_ids = jnp.arange(R, dtype=jnp.int32)[None, :]
    table_ids = jnp.arange(NQ, dtype=jnp.int32)[None, :]
    signs = jnp.array([1.0, -1.0], jnp.float32)[:, None, None, None]

    def one_block(block):
        window = lax.dynamic_slice_in_dim(padded, block.astype(jnp.int32), LAGS, 0)
        lagged = jnp.swapaxes(window[::-1], 0, 1)
        chosen = lax.dynamic_index_in_dim(weight_index, block.astype(jnp.int32), 0, keepdims=False)
        weights = jnp.sum(jnp.where(chosen[:, None] == table_ids, weight_table[None, :], jnp.float32(0.0)), axis=1)
        cut_here = lax.dynamic_index_in_dim(startup_cut, block.astype(jnp.int32), 0, keepdims=False)
        last_lag = memory[0] - 1
        kept_mask = (lag_ids < last_lag) | ((lag_ids == last_lag) & (row_ids >= cut_here))
        coef = jnp.where(kept_mask, weights[:, None], jnp.float32(0.0))
        band = lax.dynamic_index_in_dim(self_energy, block.astype(jnp.int32), 0, keepdims=False)
        scaled = band * coef[None, :, None, :] * signs
        return lax.dot_general(scaled, lagged, (((0, 1, 2), (0, 1, 2)), ((), ())), precision=lax.Precision.HIGHEST, preferred_element_type=jnp.float32)

    return lax.map(one_block, jnp.arange(NBLK, dtype=jnp.int32))
```

```python
import functools

import jax
import jax.numpy as jnp
from jax import lax
from jax.experimental import pallas as pl
from jax.experimental.pallas import tpu as pltpu
from jax.sharding import PartitionSpec as P

CHUNKS = 2
LEAST_MEMORY = 3
VMEM_LIMIT = 40 * 1024 * 1024


def split(value):
    high = value.astype(jnp.bfloat16)
    low = (value - high.astype(jnp.float32)).astype(jnp.bfloat16)
    return high, low


def product_kernel(count, has_total, scalars, *refs):
    band_refs = refs[:count]
    coef_refs = refs[count:2 * count]
    block_refs = refs[2 * count:3 * count]
    rest = refs[3 * count:]
    if has_total:
        total_ref, out_ref, high_ref, low_ref = rest
    else:
        out_ref, high_ref, low_ref = rest

    @pl.when(pl.program_id(0) == 0)
    def _():
        for q in range(count):
            high, low = split(block_refs[q][...])
            high_ref[q] = high
            low_ref[q] = low

    total = total_ref[0] if has_total else None
    for q in range(count):
        band = band_refs[q][0, :, 0]
        band = band.reshape(band.shape[0] * band.shape[1], band.shape[2]) * coef_refs[q][0]
        band_high, band_low = split(band)
        for left, right in ((high_ref[q], band_high), (low_ref[q], band_high), (high_ref[q], band_low)):
            term = jnp.dot(left, right, preferred_element_type=jnp.float32)
            total = term if total is None else total + term
    out_ref[0] = total


def products(band, coef, blocks, lags, columns, total, first, tiles):
    count = len(blocks)
    _, components, lag_count, depth, row_total = band.shape
    orb = columns.shape[0]
    rows = row_total // orb
    width = blocks[0].shape[0]
    picked = jnp.stack([jnp.asarray(lag, jnp.int32) for lag in lags])
    scalars = jnp.concatenate([jnp.minimum(picked, lag_count - 1), picked, columns[first:first + tiles]])

    def band_map(q, i, s):
        return (0, 0, s[q], 0, s[2 * count + i])

    def coef_map(q, i, s):
        return (s[count + q], 0, s[2 * count + i])

    in_specs = [pl.BlockSpec((1, components, 1, depth, rows), functools.partial(band_map, q)) for q in range(count)]
    in_specs += [pl.BlockSpec((1, 1, rows), functools.partial(coef_map, q)) for q in range(count)]
    in_specs += [pl.BlockSpec((width, components * depth), lambda i, s: (0, 0)) for _ in range(count)]
    operands = [band] * count + [coef] * count + list(blocks)
    if total is not None:
        in_specs.append(pl.BlockSpec((1, width, rows), lambda i, s: (first + i, 0, 0)))
        operands.append(total)
    in_place = total is not None and tiles == orb
    macs = count * components * depth * width * rows * tiles
    return pl.pallas_call(
        functools.partial(product_kernel, count, total is not None),
        out_shape=jax.ShapeDtypeStruct((tiles, width, rows), jnp.float32),
        grid_spec=pltpu.PrefetchScalarGridSpec(
            num_scalar_prefetch=1,
            grid=(tiles,),
            in_specs=in_specs,
            out_specs=pl.BlockSpec((1, width, rows), lambda i, s: (i, 0, 0)),
            scratch_shapes=[pltpu.VMEM((count, width, components * depth), jnp.bfloat16)] * 2,
        ),
        input_output_aliases={3 * count + 1: 0} if in_place else {},
        compiler_params=pltpu.CompilerParams(vmem_limit_bytes=VMEM_LIMIT),
        cost_estimate=pl.CostEstimate(
            flops=6 * macs, bytes_accessed=4 * tiles * rows * (count * components * depth + 2 * width), transcendentals=0
        ),
    )(scalars, *operands)


def upward(value, valid):
    devices = lax.axis_size("tm")
    return lax.ppermute(value, "tm", [(i, i + 2) for i in range(devices - 2) if valid(i)])


def exchanged(value, valid):
    devices = lax.axis_size("tm")
    return lax.ppermute(value, "tm", [(i, i ^ 1) for i in range(devices) if (i ^ 1) < devices and valid(i)])


def arrivals(block, memory, last_chunk):
    devices = lax.axis_size("tm")
    own, other = [block], []
    rounds = [[(0, 0, block)]]
    steps = memory // 2 + 1
    for t in range(steps):
        new = []
        to_odd = 2 * t + 1 < memory
        to_even = 1 <= t and 2 * t - 1 < memory
        by_shift = False
        if last_chunk and t >= 2:
            if memory % 2 == 0:
                by_shift = t == memory // 2 - 1 and devices - 2 < memory - 1
            else:
                by_shift = t == (memory - 1) // 2
        if by_shift:
            source = other[t - 1]
            even_lag = 2 * t - 1 if to_even else None
            odd_lag = 2 * t + 1 if to_odd else None

            def useful(i):
                lag = odd_lag if i % 2 else even_lag
                return lag is not None and i + 2 - lag >= 0

            got = upward(source, useful)
            new.append((even_lag, odd_lag, got))
            other.append(got)
        elif (to_odd or to_even) and t < len(own):
            got = exchanged(own[t], lambda i: i >= 2 * t and (to_even if i % 2 else to_odd))
            new.append((2 * t - 1 if to_even else None, 2 * t + 1 if to_odd else None, got))
            other.append(got)
        if 2 * (t + 1) < memory:
            got = upward(own[t], lambda i: i >= 2 * t)
            own.append(got)
            new.append((2 * t + 2, 2 * t + 2, got))
        if memory % 2 == 0 and t == memory // 2 and devices - 2 >= memory - 1:
            got = upward(other[t - 1], lambda i: i % 2 == 0 and i + 2 >= memory - 1)
            new.append((memory - 1, None, got))
        if new:
            rounds.append(new)
    return rounds


def chain(block, memory):
    devices = lax.axis_size("tm")
    rounds = [[(0, 0, block)]]
    for lag in range(1, memory):
        block = lax.ppermute(block, "tm", [(i, i + 1) for i in range(devices - 1)])
        rounds.append([(lag, lag, block)])
    return rounds


def bit_reversed(n):
    bits = n.bit_length() - 1
    return [sum(((p >> b) & 1) << (bits - 1 - b) for b in range(bits)) for p in range(n)]


def reduced(kept, sent):
    orb = lax.axis_size("orb")
    stride = 1
    while True:
        got = lax.ppermute(sent, "orb", [(i, i ^ stride) for i in range(orb)])
        half = kept.shape[0] // 2
        if half == 0:
            return kept[0] + got[0]
        sent = kept[half:] + got[half:]
        kept = kept[:half] + got[:half]
        stride *= 2


def branch(memory, band, blocks, coef):
    orb = lax.axis_size("orb")
    lag_count = band.shape[2]
    devices = lax.axis_size("tm")
    odd = lax.axis_index("tm") % 2 == 1
    power_of_two = orb & (orb - 1) == 0 and orb > 1
    order = jnp.array(bit_reversed(orb) if power_of_two else list(range(orb)), jnp.int32)
    columns = order ^ lax.axis_index("orb").astype(jnp.int32) if power_of_two else order

    def lag_of(even_lag, odd_lag):
        if even_lag == odd_lag:
            return even_lag
        none = lag_count
        return jnp.where(odd, none if odd_lag is None else odd_lag, none if even_lag is None else even_lag)

    parts = []
    plans = []
    for q, block in enumerate(blocks):
        last_chunk = q == len(blocks) - 1 and len(blocks) > 1
        plans.append(arrivals(block, memory, last_chunk) if devices % 2 == 0 else chain(block, memory))
    for rounds in plans:
        total = None
        for r, new in enumerate(rounds):
            lags = [lag_of(e, o) for e, o, _ in new]
            got = [b for _, _, b in new]
            if r < len(rounds) - 1 or not power_of_two:
                total = products(band, coef, got, lags, columns, total, 0, orb)
            else:
                sent = products(band, coef, got, lags, columns, total, orb // 2, orb // 2)
                kept = products(band, coef, got, lags, columns, total, 0, orb // 2)
        if power_of_two:
            mine = reduced(kept, sent)
        else:
            mine = lax.psum_scatter(total, "orb", scatter_dimension=0, tiled=True)[0]
        parts.append(mine.T)
    return jnp.concatenate(parts, axis=1)


def local(self_energy, history, memory, startup_cut, weight_index, weight_table):
    lag_count = self_energy.shape[2]
    row_total = self_energy.shape[4]
    table_size = weight_table.shape[0]
    lag_ids = jnp.arange(lag_count + 1, dtype=jnp.int32)[:, None]
    row_ids = jnp.arange(row_total, dtype=jnp.int32)[None, :]
    table_ids = jnp.arange(table_size, dtype=jnp.int32)[None, :]
    weights = jnp.sum(
        jnp.where(weight_index[0][:, None] == table_ids, weight_table[None, :], jnp.float32(0.0)),
        axis=1,
    )
    weights = jnp.concatenate([weights, jnp.zeros((1,), jnp.float32)])
    last_lag = memory[0] - 1
    kept_mask = (lag_ids < last_lag) | (lag_ids == last_lag) & (row_ids >= startup_cut[0])
    coef = jnp.where(kept_mask, weights[:, None], jnp.float32(0.0))[:, None, :]
    signs = jnp.array([1.0, -1.0], jnp.float32)[:, None, None]
    _, components, depth, orbitals = history.shape
    width = orbitals // CHUNKS
    blocks = [
        jnp.transpose(history[0, :, :, q * width:(q + 1) * width] * signs, (2, 0, 1)).reshape(width, components * depth)
        for q in range(CHUNKS)
    ]
    least = min(LEAST_MEMORY, lag_count)
    choices = [functools.partial(branch, kept) for kept in range(least, lag_count + 1)]
    collision = lax.switch(jnp.clip(memory[0] - least, 0, len(choices) - 1), choices, self_energy, blocks, coef)
    return collision[None]


def solution(mesh):
    in_specs = (
        P("tm", None, None, "orb", None),
        P("tm", None, "orb", None),
        P(),
        P("tm"),
        P("tm", None),
        P(),
    )
    out_specs = P("tm", "orb", None)
    return jax.shard_map(local, mesh=mesh, in_specs=in_specs, out_specs=out_specs, check_vma=False)
```

```python
import functools

import jax
import jax.numpy as jnp
from jax import lax
from jax.experimental import pallas as pl
from jax.experimental.pallas import tpu as pltpu
from jax.sharding import PartitionSpec as P

CHUNKS = 2
LEAST_MEMORY = 3
VMEM_LIMIT = 28 * 1024 * 1024


def split(value):
    high = value.astype(jnp.bfloat16)
    low = (value - high.astype(jnp.float32)).astype(jnp.bfloat16)
    return high, low


def product_kernel(count, has_total, scalars, *refs):
    band_refs = refs[:count]
    coef_refs = refs[count:2 * count]
    block_refs = refs[2 * count:3 * count]
    rest = refs[3 * count:]
    if has_total:
        total_ref, out_ref, left_ref, right_ref = rest
    else:
        out_ref, left_ref, right_ref = rest
    depth = block_refs[0].shape[1]

    @pl.when(pl.program_id(0) == 0)
    def _():
        for q in range(count):
            high, low = split(block_refs[q][...])
            for place, part in enumerate((high, low, high)):
                left_ref[:, pl.ds((3 * q + place) * depth, depth)] = part

    for q in range(count):
        band = band_refs[q][0, :, 0]
        high, low = split(band.reshape(depth, band.shape[2]) * coef_refs[q][0])
        for place, part in enumerate((high, high, low)):
            right_ref[pl.ds((3 * q + place) * depth, depth), :] = part
    term = jnp.dot(left_ref[...], right_ref[...], preferred_element_type=jnp.float32)
    out_ref[0] = total_ref[0] + term if has_total else term


def products(band, coef, blocks, lags, columns, total, first, tiles):
    count = len(blocks)
    _, components, lag_count, depth, row_total = band.shape
    orb = columns.shape[0]
    rows = row_total // orb
    width = blocks[0].shape[0]
    picked = jnp.stack([jnp.asarray(lag, jnp.int32) for lag in lags])
    scalars = jnp.concatenate([jnp.minimum(picked, lag_count - 1), picked, columns[first:first + tiles]])

    def band_map(q, i, s):
        return (0, 0, s[q], 0, s[2 * count + i])

    def coef_map(q, i, s):
        return (s[count + q], 0, s[2 * count + i])

    in_specs = [pl.BlockSpec((1, components, 1, depth, rows), functools.partial(band_map, q)) for q in range(count)]
    in_specs += [pl.BlockSpec((1, 1, rows), functools.partial(coef_map, q)) for q in range(count)]
    in_specs += [pl.BlockSpec((width, components * depth), lambda i, s: (0, 0)) for _ in range(count)]
    operands = [band] * count + [coef] * count + list(blocks)
    if total is not None:
        in_specs.append(pl.BlockSpec((1, width, rows), lambda i, s: (first + i, 0, 0)))
        operands.append(total)
    in_place = total is not None and tiles == orb
    return pl.pallas_call(
        functools.partial(product_kernel, count, total is not None),
        out_shape=jax.ShapeDtypeStruct((tiles, width, rows), jnp.float32),
        grid_spec=pltpu.PrefetchScalarGridSpec(
            num_scalar_prefetch=1,
            grid=(tiles,),
            in_specs=in_specs,
            out_specs=pl.BlockSpec((1, width, rows), lambda i, s: (i, 0, 0)),
            scratch_shapes=[
                pltpu.VMEM((width, 3 * count * components * depth), jnp.bfloat16),
                pltpu.VMEM((3 * count * components * depth, rows), jnp.bfloat16),
            ],
        ),
        input_output_aliases={3 * count + 1: 0} if in_place else {},
        compiler_params=pltpu.CompilerParams(vmem_limit_bytes=VMEM_LIMIT),
        cost_estimate=pl.CostEstimate(flops=1024, bytes_accessed=1024, transcendentals=0),
    )(scalars, *operands)


def upward(value, valid):
    devices = lax.axis_size("tm")
    return lax.ppermute(value, "tm", [(i, i + 2) for i in range(devices - 2) if valid(i)])


def exchanged(value, valid):
    devices = lax.axis_size("tm")
    return lax.ppermute(value, "tm", [(i, i ^ 1) for i in range(devices) if (i ^ 1) < devices and valid(i)])


def after(value, *earlier):
    return lax.optimization_barrier((value,) + earlier)[0]


def moves(t, own, other, memory, by_shift, gate):
    devices = lax.axis_size("tm")
    new = []
    to_odd = 2 * t + 1 < memory
    to_even = 1 <= t and 2 * t - 1 < memory
    even_lag = 2 * t - 1 if to_even else None
    odd_lag = 2 * t + 1 if to_odd else None
    if 2 * (t + 1) < memory:
        got = upward(after(own[t], *gate), lambda i: i >= 2 * t)
        own.append(got)
        new.append((2 * t + 2, 2 * t + 2, got))
    if by_shift:

        def useful(i):
            lag = odd_lag if i % 2 else even_lag
            return lag is not None and i + 2 - lag >= 0

        got = upward(after(other[t - 1], *gate), useful)
        other.append(got)
        new.append((even_lag, odd_lag, got))
    elif (to_odd or to_even) and t < len(own):
        got = exchanged(after(own[t], *gate), lambda i: i >= 2 * t and (to_even if i % 2 else to_odd))
        other.append(got)
        new.append((even_lag, odd_lag, got))
    if memory % 2 == 0 and t == memory // 2 and devices - 2 >= memory - 1:
        got = upward(after(other[t - 1], *gate), lambda i: i % 2 == 0 and i + 2 >= memory - 1)
        new.append((memory - 1, None, got))
    return new


def shift_round(memory):
    if memory % 2:
        t = (memory - 1) // 2
    else:
        t = memory // 2 - 1 if lax.axis_size("tm") - 2 < memory - 1 else 0
    return t if t >= 2 else None


def next_in_chain(t, own, memory, gate):
    devices = lax.axis_size("tm")
    if t + 1 >= memory:
        return []
    got = lax.ppermute(after(own[t], *gate), "tm", [(i, i + 1) for i in range(devices - 1)])
    own.append(got)
    return [(t + 1, t + 1, got)]


def bit_reversed(n):
    bits = n.bit_length() - 1
    return [sum(((p >> b) & 1) << (bits - 1 - b) for b in range(bits)) for p in range(n)]


def branch(memory, band, blocks, coef):
    orb = lax.axis_size("orb")
    lag_count = band.shape[2]
    paired = lax.axis_size("tm") % 2 == 0
    odd = lax.axis_index("tm") % 2 == 1
    power_of_two = orb & (orb - 1) == 0 and orb > 1
    order = jnp.array(bit_reversed(orb) if power_of_two else list(range(orb)), jnp.int32)
    columns = order ^ lax.axis_index("orb").astype(jnp.int32) if power_of_two else order
    count = len(blocks)
    own = [[block] for block in blocks]
    other = [[] for _ in blocks]
    arrived = [[[(0, 0, block)]] for block in blocks]
    totals = [None] * count

    def lag_of(even_lag, odd_lag):
        if even_lag == odd_lag:
            return even_lag
        none = lag_count
        return jnp.where(odd, none if odd_lag is None else odd_lag, none if even_lag is None else even_lag)

    def receive(t, q, gate):
        if paired:
            by_shift = t == shift_round(memory) and count > 2 and q >= (count + 1) // 2
            new = moves(t, own[q], other[q], memory, by_shift, gate)
        else:
            new = next_in_chain(t, own[q], memory, gate)
        if new:
            arrived[q].append(new)
        return bool(new)

    def multiply(r, q, first, tiles, total):
        new = arrived[q][r]
        lags = [lag_of(e, o) for e, o, _ in new]
        return products(band, coef, [b for _, _, b in new], lags, columns, total, first, tiles)

    gate = ()
    round_at = 0
    more = True
    while more:
        more = False
        for q in range(count):
            together = tuple(b for _, _, b in arrived[q][-1])
            more = receive(round_at, q, gate + together) or more
            if round_at + 1 < len(arrived[q]):
                totals[q] = multiply(round_at, q, 0, orb, totals[q])
                if round_at > 0 or q == count - 1:
                    gate = (totals[q],)
        round_at += 1

    parts = []
    sending = arriving = None
    for q in range(count):
        r = len(arrived[q]) - 1
        if not power_of_two:
            total = multiply(r, q, 0, orb, totals[q])
            parts.append(lax.psum_scatter(total, "orb", scatter_dimension=0, tiled=True)[0].T)
            continue
        if sending is not None:
            totals[q] = after(totals[q], sending)
        elif count > 1:
            totals[q] = after(totals[q], *gate)
        sent = multiply(r, q, orb // 2, orb // 2, totals[q])
        kept = multiply(r, q, 0, orb // 2, totals[q])
        stride = 1
        while True:
            sending = sent
            got = lax.ppermute(sent, "orb", [(i, i ^ stride) for i in range(orb)])
            half = kept.shape[0] // 2
            if half == 0:
                break
            sent = kept[half:] + got[half:]
            kept = kept[:half] + got[:half]
            stride *= 2
            if arriving is not None:
                sent = after(sent, arriving)
        arriving = got
        parts.append((kept[0] + got[0]).T)
    return jnp.concatenate(parts, axis=1)


def local(self_energy, history, memory, startup_cut, weight_index, weight_table):
    lag_count = self_energy.shape[2]
    row_total = self_energy.shape[4]
    table_size = weight_table.shape[0]
    lag_ids = jnp.arange(lag_count + 1, dtype=jnp.int32)[:, None]
    row_ids = jnp.arange(row_total, dtype=jnp.int32)[None, :]
    table_ids = jnp.arange(table_size, dtype=jnp.int32)[None, :]
    weights = jnp.sum(
        jnp.where(weight_index[0][:, None] == table_ids, weight_table[None, :], jnp.float32(0.0)),
        axis=1,
    )
    weights = jnp.concatenate([weights, jnp.zeros((1,), jnp.float32)])
    last_lag = memory[0] - 1
    kept_mask = (lag_ids < last_lag) | (lag_ids == last_lag) & (row_ids >= startup_cut[0])
    coef = jnp.where(kept_mask, weights[:, None], jnp.float32(0.0))[:, None, :]
    signs = jnp.array([1.0, -1.0], jnp.float32)[:, None, None]
    _, components, depth, orbitals = history.shape
    width = orbitals // CHUNKS
    blocks = [
        jnp.transpose(history[0, :, :, q * width:(q + 1) * width] * signs, (2, 0, 1)).reshape(width, components * depth)
        for q in range(CHUNKS)
    ]
    least = min(LEAST_MEMORY, lag_count)
    choices = [functools.partial(branch, kept) for kept in range(least, lag_count + 1)]
    collision = lax.switch(jnp.clip(memory[0] - least, 0, len(choices) - 1), choices, self_energy, blocks, coef)
    return collision[None]


def solution(mesh):
    in_specs = (
        P("tm", None, None, "orb", None),
        P("tm", None, "orb", None),
        P(),
        P("tm"),
        P("tm", None),
        P(),
    )
    out_specs = P("tm", "orb", None)
    return jax.shard_map(local, mesh=mesh, in_specs=in_specs, out_specs=out_specs, check_vma=False)
```

```python
import functools

import jax
import jax.numpy as jnp
from jax import lax
from jax.experimental import pallas as pl
from jax.experimental.pallas import tpu as pltpu
from jax.sharding import PartitionSpec as P

CHUNKS = 4
LEAST_MEMORY = 3
VMEM_LIMIT = 58 * 1024 * 1024


def split(value):
    high = value.astype(jnp.bfloat16)
    low = (value - high.astype(jnp.float32)).astype(jnp.bfloat16)
    return high, low


def product_kernel(count, has_total, scalars, *refs):
    band_refs = refs[:count]
    coef_refs = refs[count:2 * count]
    block_refs = refs[2 * count:3 * count]
    rest = refs[3 * count:]
    if has_total:
        total_ref, out_ref, left_ref, right_ref = rest
    else:
        out_ref, left_ref, right_ref = rest
    depth = block_refs[0].shape[1]

    @pl.when(pl.program_id(0) == 0)
    def _():
        for q in range(count):
            high, low = split(block_refs[q][...])
            for place, part in enumerate((high, low, high)):
                left_ref[:, pl.ds((3 * q + place) * depth, depth)] = part

    for q in range(count):
        band = band_refs[q][0, :, 0]
        high, low = split(band.reshape(depth, band.shape[2]) * coef_refs[q][0])
        for place, part in enumerate((high, high, low)):
            right_ref[pl.ds((3 * q + place) * depth, depth), :] = part
    term = jnp.dot(left_ref[...], right_ref[...], preferred_element_type=jnp.float32)
    out_ref[0] = total_ref[0] + term if has_total else term


def products(band, coef, blocks, lags, columns, total, first, tiles):
    count = len(blocks)
    _, components, lag_count, depth, row_total = band.shape
    orb = columns.shape[0]
    rows = row_total // orb
    width = blocks[0].shape[0]
    picked = jnp.stack([jnp.asarray(lag, jnp.int32) for lag in lags])
    scalars = jnp.concatenate([jnp.minimum(picked, lag_count - 1), picked, columns[first:first + tiles]])

    def band_map(q, i, s):
        return (0, 0, s[q], 0, s[2 * count + i])

    def coef_map(q, i, s):
        return (s[count + q], 0, s[2 * count + i])

    in_specs = [pl.BlockSpec((1, components, 1, depth, rows), functools.partial(band_map, q)) for q in range(count)]
    in_specs += [pl.BlockSpec((1, 1, rows), functools.partial(coef_map, q)) for q in range(count)]
    in_specs += [pl.BlockSpec((width, components * depth), lambda i, s: (0, 0)) for _ in range(count)]
    operands = [band] * count + [coef] * count + list(blocks)
    if total is not None:
        in_specs.append(pl.BlockSpec((1, width, rows), lambda i, s: (first + i, 0, 0)))
        operands.append(total)
    in_place = total is not None and tiles == orb
    return pl.pallas_call(
        functools.partial(product_kernel, count, total is not None),
        out_shape=jax.ShapeDtypeStruct((tiles, width, rows), jnp.float32),
        grid_spec=pltpu.PrefetchScalarGridSpec(
            num_scalar_prefetch=1,
            grid=(tiles,),
            in_specs=in_specs,
            out_specs=pl.BlockSpec((1, width, rows), lambda i, s: (i, 0, 0)),
            scratch_shapes=[
                pltpu.VMEM((width, 3 * count * components * depth), jnp.bfloat16),
                pltpu.VMEM((3 * count * components * depth, rows), jnp.bfloat16),
            ],
        ),
        input_output_aliases={3 * count + 1: 0} if in_place else {},
        compiler_params=pltpu.CompilerParams(vmem_limit_bytes=VMEM_LIMIT),
        cost_estimate=pl.CostEstimate(flops=1024, bytes_accessed=1024, transcendentals=0),
    )(scalars, *operands)


def upward(value, valid):
    devices = lax.axis_size("tm")
    return lax.ppermute(value, "tm", [(i, i + 2) for i in range(devices - 2) if valid(i)])


def exchanged(value, valid):
    devices = lax.axis_size("tm")
    return lax.ppermute(value, "tm", [(i, i ^ 1) for i in range(devices) if (i ^ 1) < devices and valid(i)])


def after(value, *earlier):
    return lax.optimization_barrier((value,) + earlier)[0]


def moves(t, own, other, memory, by_shift, gate):
    devices = lax.axis_size("tm")
    new = []
    to_odd = 2 * t + 1 < memory
    to_even = 1 <= t and 2 * t - 1 < memory
    even_lag = 2 * t - 1 if to_even else None
    odd_lag = 2 * t + 1 if to_odd else None
    if 2 * (t + 1) < memory:
        got = upward(after(own[t], *gate), lambda i: i >= 2 * t)
        own.append(got)
        new.append((2 * t + 2, 2 * t + 2, got))
    if by_shift:

        def useful(i):
            lag = odd_lag if i % 2 else even_lag
            return lag is not None and i + 2 - lag >= 0

        got = upward(after(other[t - 1], *gate), useful)
        other.append(got)
        new.append((even_lag, odd_lag, got))
    elif (to_odd or to_even) and t < len(own):
        got = exchanged(after(own[t], *gate), lambda i: i >= 2 * t and (to_even if i % 2 else to_odd))
        other.append(got)
        new.append((even_lag, odd_lag, got))
    if memory % 2 == 0 and t == memory // 2 and devices - 2 >= memory - 1:
        got = upward(after(other[t - 1], *gate), lambda i: i % 2 == 0 and i + 2 >= memory - 1)
        new.append((memory - 1, None, got))
    return new


def shift_round(memory):
    if memory % 2:
        t = (memory - 1) // 2
    else:
        t = memory // 2 - 1 if lax.axis_size("tm") - 2 < memory - 1 else 0
    return t if t >= 2 else None


def next_in_chain(t, own, memory, gate):
    devices = lax.axis_size("tm")
    if t + 1 >= memory:
        return []
    got = lax.ppermute(after(own[t], *gate), "tm", [(i, i + 1) for i in range(devices - 1)])
    own.append(got)
    return [(t + 1, t + 1, got)]


def bit_reversed(n):
    bits = n.bit_length() - 1
    return [sum(((p >> b) & 1) << (bits - 1 - b) for b in range(bits)) for p in range(n)]


def branch(memory, band, blocks, coef):
    orb = lax.axis_size("orb")
    lag_count = band.shape[2]
    paired = lax.axis_size("tm") % 2 == 0
    odd = lax.axis_index("tm") % 2 == 1
    power_of_two = orb & (orb - 1) == 0 and orb > 1
    order = jnp.array(bit_reversed(orb) if power_of_two else list(range(orb)), jnp.int32)
    columns = order ^ lax.axis_index("orb").astype(jnp.int32) if power_of_two else order
    count = len(blocks)
    own = [[block] for block in blocks]
    other = [[] for _ in blocks]
    arrived = [[[(0, 0, block)]] for block in blocks]
    totals = [None] * count

    def lag_of(even_lag, odd_lag):
        if even_lag == odd_lag:
            return even_lag
        none = lag_count
        return jnp.where(odd, none if odd_lag is None else odd_lag, none if even_lag is None else even_lag)

    def receive(t, q, gate):
        if paired:
            by_shift = t == shift_round(memory) and count > 2 and q >= (count + 1) // 2
            new = moves(t, own[q], other[q], memory, by_shift, gate)
        else:
            new = next_in_chain(t, own[q], memory, gate)
        if new:
            arrived[q].append(new)
        return bool(new)

    def multiply(r, q, first, tiles, total):
        new = arrived[q][r]
        lags = [lag_of(e, o) for e, o, _ in new]
        return products(band, coef, [b for _, _, b in new], lags, columns, total, first, tiles)

    gate = ()
    round_at = 0
    more = True
    while more:
        more = False
        for q in range(count):
            together = tuple(b for _, _, b in arrived[q][-1])
            more = receive(round_at, q, gate + together) or more
            if round_at + 1 < len(arrived[q]):
                totals[q] = multiply(round_at, q, 0, orb, totals[q])
                if round_at > 0 or q == count - 1:
                    gate = (totals[q],)
        round_at += 1

    parts = []
    sending = arriving = None
    for q in range(count):
        r = len(arrived[q]) - 1
        if not power_of_two:
            total = multiply(r, q, 0, orb, totals[q])
            parts.append(lax.psum_scatter(total, "orb", scatter_dimension=0, tiled=True)[0].T)
            continue
        if sending is not None:
            totals[q] = after(totals[q], sending)
        elif count > 1:
            totals[q] = after(totals[q], *gate)
        sent = multiply(r, q, orb // 2, orb // 2, totals[q])
        kept = multiply(r, q, 0, orb // 2, totals[q])
        stride = 1
        while True:
            sending = sent
            got = lax.ppermute(sent, "orb", [(i, i ^ stride) for i in range(orb)])
            half = kept.shape[0] // 2
            if half == 0:
                break
            sent = kept[half:] + got[half:]
            kept = kept[:half] + got[:half]
            stride *= 2
            if arriving is not None:
                sent = after(sent, arriving)
        arriving = got
        parts.append((kept[0] + got[0]).T)
    return jnp.concatenate(parts, axis=1)


def local(self_energy, history, memory, startup_cut, weight_index, weight_table):
    lag_count = self_energy.shape[2]
    row_total = self_energy.shape[4]
    table_size = weight_table.shape[0]
    lag_ids = jnp.arange(lag_count + 1, dtype=jnp.int32)[:, None]
    row_ids = jnp.arange(row_total, dtype=jnp.int32)[None, :]
    table_ids = jnp.arange(table_size, dtype=jnp.int32)[None, :]
    weights = jnp.sum(
        jnp.where(weight_index[0][:, None] == table_ids, weight_table[None, :], jnp.float32(0.0)),
        axis=1,
    )
    weights = jnp.concatenate([weights, jnp.zeros((1,), jnp.float32)])
    last_lag = memory[0] - 1
    kept_mask = (lag_ids < last_lag) | (lag_ids == last_lag) & (row_ids >= startup_cut[0])
    coef = jnp.where(kept_mask, weights[:, None], jnp.float32(0.0))[:, None, :]
    signs = jnp.array([1.0, -1.0], jnp.float32)[:, None, None]
    _, components, depth, orbitals = history.shape
    width = orbitals // CHUNKS
    blocks = [
        jnp.transpose(history[0, :, :, q * width:(q + 1) * width] * signs, (2, 0, 1)).reshape(width, components * depth)
        for q in range(CHUNKS)
    ]
    least = min(LEAST_MEMORY, lag_count)
    choices = [functools.partial(branch, kept) for kept in range(least, lag_count + 1)]
    collision = lax.switch(jnp.clip(memory[0] - least, 0, len(choices) - 1), choices, self_energy, blocks, coef)
    return collision[None]


def solution(mesh):
    in_specs = (
        P("tm", None, None, "orb", None),
        P("tm", None, "orb", None),
        P(),
        P("tm"),
        P("tm", None),
        P(),
    )
    out_specs = P("tm", "orb", None)
    return jax.shard_map(local, mesh=mesh, in_specs=in_specs, out_specs=out_specs, check_vma=False)
```

```python
import functools

import jax
import jax.numpy as jnp
from jax import lax
from jax.experimental import pallas as pl
from jax.experimental.pallas import tpu as pltpu
from jax.sharding import PartitionSpec as P

CHUNKS = 2
LEAST_MEMORY = 3
STEP = 64
SPAN = 256
VMEM_LIMIT = 58 * 1024 * 1024


def split(value):
    high = value.astype(jnp.bfloat16)
    low = (value - high.astype(jnp.float32)).astype(jnp.bfloat16)
    return high, low


def product_kernel(count, has_total, scalars, *refs):
    band_refs = refs[:count]
    coef_refs = refs[count:2 * count]
    block_refs = refs[2 * count:3 * count]
    rest = refs[3 * count:]
    if has_total:
        total_ref, out_ref, left_ref, right_ref = rest
    else:
        out_ref, left_ref, right_ref = rest
    depth = block_refs[0].shape[1]

    width = block_refs[0].shape[0]
    rows = band_refs[0].shape[4]
    band_step = STEP if band_refs[0].shape[3] % STEP == 0 else band_refs[0].shape[3]
    band_steps = band_refs[0].shape[3] // band_step
    block_step = STEP if width % STEP == 0 else width

    @pl.when(pl.program_id(0) == 0)
    def _():
        for q in range(count):

            @pl.loop(0, width // block_step)
            def _(step):
                at = pl.ds(pl.multiple_of(step * block_step, block_step), block_step)
                high, low = split(block_refs[q][at, :])
                for place, part in enumerate((high, low, high)):
                    left_ref[at, pl.ds((3 * q + place) * depth, depth)] = part

    for q in range(count):

        @pl.loop(0, depth // band_step)
        def _(step):
            inner = pl.multiple_of(lax.rem(step, band_steps) * band_step, band_step)
            high, low = split(band_refs[q][0, lax.div(step, band_steps), 0, pl.ds(inner, band_step), :] * coef_refs[q][0])
            for place, part in enumerate((high, high, low)):
                at = pl.multiple_of((3 * q + place) * depth + step * band_step, band_step)
                right_ref[pl.ds(at, band_step), :] = part

    across = SPAN if rows % SPAN == 0 else rows

    @pl.loop(0, rows // across)
    def _(step):
        at = pl.ds(pl.multiple_of(step * across, across), across)
        term = jnp.dot(left_ref[...], right_ref[:, at], preferred_element_type=jnp.float32)
        out_ref[0, :, at] = total_ref[0, :, at] + term if has_total else term


def products(band, coef, blocks, lags, columns, total, first, tiles):
    count = len(blocks)
    _, components, lag_count, depth, row_total = band.shape
    orb = columns.shape[0]
    rows = row_total // orb
    width = blocks[0].shape[0]
    picked = jnp.stack([jnp.asarray(lag, jnp.int32) for lag in lags])
    scalars = jnp.concatenate([jnp.minimum(picked, lag_count - 1), picked, columns[first:first + tiles]])

    def band_map(q, i, s):
        return (0, 0, s[q], 0, s[2 * count + i])

    def coef_map(q, i, s):
        return (s[count + q], 0, s[2 * count + i])

    in_specs = [pl.BlockSpec((1, components, 1, depth, rows), functools.partial(band_map, q)) for q in range(count)]
    in_specs += [pl.BlockSpec((1, 1, rows), functools.partial(coef_map, q)) for q in range(count)]
    in_specs += [pl.BlockSpec((width, components * depth), lambda i, s: (0, 0)) for _ in range(count)]
    operands = [band] * count + [coef] * count + list(blocks)
    if total is not None:
        in_specs.append(pl.BlockSpec((1, width, rows), lambda i, s: (first + i, 0, 0)))
        operands.append(total)
    in_place = total is not None and tiles == orb
    return pl.pallas_call(
        functools.partial(product_kernel, count, total is not None),
        out_shape=jax.ShapeDtypeStruct((tiles, width, rows), jnp.float32),
        grid_spec=pltpu.PrefetchScalarGridSpec(
            num_scalar_prefetch=1,
            grid=(tiles,),
            in_specs=in_specs,
            out_specs=pl.BlockSpec((1, width, rows), lambda i, s: (i, 0, 0)),
            scratch_shapes=[
                pltpu.VMEM((width, 3 * count * components * depth), jnp.bfloat16),
                pltpu.VMEM((3 * count * components * depth, rows), jnp.bfloat16),
            ],
        ),
        input_output_aliases={3 * count + 1: 0} if in_place else {},
        compiler_params=pltpu.CompilerParams(vmem_limit_bytes=VMEM_LIMIT),
        cost_estimate=pl.CostEstimate(flops=1024, bytes_accessed=1024, transcendentals=0),
    )(scalars, *operands)


def upward(value, valid):
    devices = lax.axis_size("tm")
    return lax.ppermute(value, "tm", [(i, i + 2) for i in range(devices - 2) if valid(i)])


def exchanged(value, valid):
    devices = lax.axis_size("tm")
    return lax.ppermute(value, "tm", [(i, i ^ 1) for i in range(devices) if (i ^ 1) < devices and valid(i)])


def after(value, *earlier):
    return lax.optimization_barrier((value,) + earlier)[0]


def moves(t, own, other, memory, by_shift, gate):
    devices = lax.axis_size("tm")
    new = []
    to_odd = 2 * t + 1 < memory
    to_even = 1 <= t and 2 * t - 1 < memory
    even_lag = 2 * t - 1 if to_even else None
    odd_lag = 2 * t + 1 if to_odd else None
    if 2 * (t + 1) < memory:
        got = upward(after(own[t], *gate), lambda i: i >= 2 * t)
        own.append(got)
        new.append((2 * t + 2, 2 * t + 2, got))
    if by_shift:

        def useful(i):
            lag = odd_lag if i % 2 else even_lag
            return lag is not None and i + 2 - lag >= 0

        got = upward(after(other[t - 1], *gate), useful)
        other.append(got)
        new.append((even_lag, odd_lag, got))
    elif (to_odd or to_even) and t < len(own):
        got = exchanged(after(own[t], *gate), lambda i: i >= 2 * t and (to_even if i % 2 else to_odd))
        other.append(got)
        new.append((even_lag, odd_lag, got))
    if memory % 2 == 0 and t == memory // 2 and devices - 2 >= memory - 1:
        got = upward(after(other[t - 1], *gate), lambda i: i % 2 == 0 and i + 2 >= memory - 1)
        new.append((memory - 1, None, got))
    return new


def shift_round(memory):
    if memory % 2:
        t = (memory - 1) // 2
    else:
        t = memory // 2 - 1 if lax.axis_size("tm") - 2 < memory - 1 else 0
    return t if t >= 2 else None


def next_in_chain(t, own, memory, gate):
    devices = lax.axis_size("tm")
    if t + 1 >= memory:
        return []
    got = lax.ppermute(after(own[t], *gate), "tm", [(i, i + 1) for i in range(devices - 1)])
    own.append(got)
    return [(t + 1, t + 1, got)]


def bit_reversed(n):
    bits = n.bit_length() - 1
    return [sum(((p >> b) & 1) << (bits - 1 - b) for b in range(bits)) for p in range(n)]


def branch(memory, band, blocks, coef):
    orb = lax.axis_size("orb")
    lag_count = band.shape[2]
    paired = lax.axis_size("tm") % 2 == 0
    odd = lax.axis_index("tm") % 2 == 1
    power_of_two = orb & (orb - 1) == 0 and orb > 1
    order = jnp.array(bit_reversed(orb) if power_of_two else list(range(orb)), jnp.int32)
    columns = order ^ lax.axis_index("orb").astype(jnp.int32) if power_of_two else order
    count = len(blocks)
    own = [[block] for block in blocks]
    other = [[] for _ in blocks]
    arrived = [[[(0, 0, block)]] for block in blocks]
    totals = [None] * count

    def lag_of(even_lag, odd_lag):
        if even_lag == odd_lag:
            return even_lag
        none = lag_count
        return jnp.where(odd, none if odd_lag is None else odd_lag, none if even_lag is None else even_lag)

    def receive(t, q, gate):
        if paired:
            by_shift = t == shift_round(memory) and count > 2 and q >= (count + 1) // 2
            new = moves(t, own[q], other[q], memory, by_shift, gate)
        else:
            new = next_in_chain(t, own[q], memory, gate)
        if new:
            arrived[q].append(new)
        return bool(new)

    def multiply(r, q, first, tiles, total):
        new = arrived[q][r]
        lags = [lag_of(e, o) for e, o, _ in new]
        return products(band, coef, [b for _, _, b in new], lags, columns, total, first, tiles)

    gate = ()
    round_at = 0
    more = True
    while more:
        more = False
        for q in range(count):
            together = tuple(b for _, _, b in arrived[q][-1])
            more = receive(round_at, q, gate + together) or more
            if round_at + 1 < len(arrived[q]):
                totals[q] = multiply(round_at, q, 0, orb, totals[q])
                if round_at > 0 or q == count - 1:
                    gate = (totals[q],)
        round_at += 1

    parts = []
    arriving = None
    for q in range(count):
        r = len(arrived[q]) - 1
        if not power_of_two:
            total = multiply(r, q, 0, orb, totals[q])
            parts.append(lax.psum_scatter(total, "orb", scatter_dimension=0, tiled=True)[0].T)
            continue
        if arriving is not None:
            totals[q] = after(totals[q], arriving)
        elif count > 1:
            totals[q] = after(totals[q], *gate)
        sent = multiply(r, q, orb // 2, orb // 2, totals[q])
        kept = multiply(r, q, 0, orb // 2, totals[q])
        stride = 1
        while True:
            got = lax.ppermute(sent, "orb", [(i, i ^ stride) for i in range(orb)])
            half = kept.shape[0] // 2
            if half == 0:
                break
            sent = kept[half:] + got[half:]
            kept = kept[:half] + got[:half]
            stride *= 2
        arriving = got
        parts.append((kept[0] + got[0]).T)
    return jnp.concatenate(parts, axis=1)


def local(self_energy, history, memory, startup_cut, weight_index, weight_table):
    lag_count = self_energy.shape[2]
    row_total = self_energy.shape[4]
    table_size = weight_table.shape[0]
    lag_ids = jnp.arange(lag_count + 1, dtype=jnp.int32)[:, None]
    row_ids = jnp.arange(row_total, dtype=jnp.int32)[None, :]
    table_ids = jnp.arange(table_size, dtype=jnp.int32)[None, :]
    weights = jnp.sum(
        jnp.where(weight_index[0][:, None] == table_ids, weight_table[None, :], jnp.float32(0.0)),
        axis=1,
    )
    weights = jnp.concatenate([weights, jnp.zeros((1,), jnp.float32)])
    last_lag = memory[0] - 1
    kept_mask = (lag_ids < last_lag) | (lag_ids == last_lag) & (row_ids >= startup_cut[0])
    coef = jnp.where(kept_mask, weights[:, None], jnp.float32(0.0))[:, None, :]
    signs = jnp.array([1.0, -1.0], jnp.float32)[:, None, None]
    _, components, depth, orbitals = history.shape
    width = orbitals // CHUNKS
    blocks = [
        jnp.transpose(history[0, :, :, q * width:(q + 1) * width] * signs, (2, 0, 1)).reshape(width, components * depth)
        for q in range(CHUNKS)
    ]
    least = min(LEAST_MEMORY, lag_count)
    choices = [functools.partial(branch, kept) for kept in range(least, lag_count + 1)]
    collision = lax.switch(jnp.clip(memory[0] - least, 0, len(choices) - 1), choices, self_energy, blocks, coef)
    return collision[None]


def solution(mesh):
    in_specs = (
        P("tm", None, None, "orb", None),
        P("tm", None, "orb", None),
        P(),
        P("tm"),
        P("tm", None),
        P(),
    )
    out_specs = P("tm", "orb", None)
    return jax.shard_map(local, mesh=mesh, in_specs=in_specs, out_specs=out_specs, check_vma=False)
```

```python
import functools

import jax
import jax.numpy as jnp
from jax import lax
from jax.experimental import pallas as pl
from jax.experimental.pallas import tpu as pltpu
from jax.sharding import PartitionSpec as P

CHUNKS = 2
LEAST_MEMORY = 3
STEP = 64
SPAN = 256
SPLIT_SPAN = 512
VMEM_LIMIT = 58 * 1024 * 1024


def split(value):
    high = value.astype(jnp.bfloat16)
    low = (value - high.astype(jnp.float32)).astype(jnp.bfloat16)
    return high, low


def split_kernel(band_ref, coef_ref, out_ref):
    components, depth = band_ref.shape[1], band_ref.shape[3]
    for c in range(components):
        high, low = split(band_ref[0, c, 0] * coef_ref[0])
        out_ref[0, 0, pl.ds(c * depth, depth), :] = high
        out_ref[0, 1, pl.ds(c * depth, depth), :] = low


def weighted(band, coef, lags):
    _, components, _, depth, row_total = band.shape
    span = SPLIT_SPAN if row_total % SPLIT_SPAN == 0 else row_total
    return pl.pallas_call(
        split_kernel,
        out_shape=jax.ShapeDtypeStruct((lags, 2, components * depth, row_total), jnp.bfloat16),
        grid=(lags, row_total // span),
        in_specs=[
            pl.BlockSpec((1, components, 1, depth, span), lambda l, i: (0, 0, l, 0, i)),
            pl.BlockSpec((1, 1, span), lambda l, i: (l, 0, i)),
        ],
        out_specs=pl.BlockSpec((1, 2, components * depth, span), lambda l, i: (l, 0, 0, i)),
        compiler_params=pltpu.CompilerParams(vmem_limit_bytes=VMEM_LIMIT),
        cost_estimate=pl.CostEstimate(flops=1024, bytes_accessed=1024, transcendentals=0),
    )(band, coef)


def product_kernel(count, has_total, scalars, *refs):
    band_refs = refs[:count]
    block_refs = refs[count:2 * count]
    rest = refs[2 * count:]
    if has_total:
        total_ref, out_ref, left_ref = rest
    else:
        out_ref, left_ref = rest
    width, depth = block_refs[0].shape
    block_step = STEP if width % STEP == 0 else width

    @pl.when(pl.program_id(0) == 0)
    def _():
        for q in range(count):

            @pl.loop(0, width // block_step)
            def _(step):
                at = pl.ds(pl.multiple_of(step * block_step, block_step), block_step)
                high, low = split(block_refs[q][at, :])
                for place, part in enumerate((high, high, low)):
                    left_ref[q, at, pl.ds(place * depth, depth)] = part

    total = total_ref[0] if has_total else None
    for q in range(count):
        both = band_refs[q][0].reshape(2 * depth, out_ref.shape[2])
        term = jnp.dot(left_ref[q, :, :2 * depth], both, preferred_element_type=jnp.float32)
        term = term + jnp.dot(left_ref[q, :, 2 * depth:], band_refs[q][0, 0], preferred_element_type=jnp.float32)
        total = term if total is None else total + term
    out_ref[0] = total


def products(band, blocks, lags, columns, total, first, tiles):
    count = len(blocks)
    lag_count, _, depth, row_total = band.shape
    orb = columns.shape[0]
    rows = row_total // orb
    span = SPAN if rows % SPAN == 0 else rows
    cuts = rows // span
    width = blocks[0].shape[0]
    picked = jnp.stack([jnp.asarray(lag, jnp.int32) for lag in lags])
    scalars = jnp.concatenate([jnp.minimum(picked, lag_count - 1), columns[first:first + tiles]])

    def band_map(q, i, p, s):
        return (s[q], 0, 0, s[count + i] * cuts + p)

    in_specs = [pl.BlockSpec((1, 2, depth, span), functools.partial(band_map, q)) for q in range(count)]
    in_specs += [pl.BlockSpec((width, depth), lambda i, p, s: (0, 0)) for _ in range(count)]
    operands = [band] * count + list(blocks)
    if total is not None:
        in_specs.append(pl.BlockSpec((1, width, span), lambda i, p, s: (first + i, 0, p)))
        operands.append(total)
    in_place = total is not None and tiles == orb
    return pl.pallas_call(
        functools.partial(product_kernel, count, total is not None),
        out_shape=jax.ShapeDtypeStruct((tiles, width, rows), jnp.float32),
        grid_spec=pltpu.PrefetchScalarGridSpec(
            num_scalar_prefetch=1,
            grid=(tiles, cuts),
            in_specs=in_specs,
            out_specs=pl.BlockSpec((1, width, span), lambda i, p, s: (i, 0, p)),
            scratch_shapes=[pltpu.VMEM((count, width, 3 * depth), jnp.bfloat16)],
        ),
        input_output_aliases={2 * count + 1: 0} if in_place else {},
        compiler_params=pltpu.CompilerParams(vmem_limit_bytes=VMEM_LIMIT),
        cost_estimate=pl.CostEstimate(flops=1024, bytes_accessed=1024, transcendentals=0),
    )(scalars, *operands)


def upward(value, valid):
    devices = lax.axis_size("tm")
    return lax.ppermute(value, "tm", [(i, i + 2) for i in range(devices - 2) if valid(i)])


def exchanged(value, valid):
    devices = lax.axis_size("tm")
    return lax.ppermute(value, "tm", [(i, i ^ 1) for i in range(devices) if (i ^ 1) < devices and valid(i)])


def after(value, *earlier):
    return lax.optimization_barrier((value,) + earlier)[0]


def moves(t, own, other, memory, by_shift, gate):
    devices = lax.axis_size("tm")
    new = []
    to_odd = 2 * t + 1 < memory
    to_even = 1 <= t and 2 * t - 1 < memory
    even_lag = 2 * t - 1 if to_even else None
    odd_lag = 2 * t + 1 if to_odd else None
    if 2 * (t + 1) < memory:
        got = upward(after(own[t], *gate), lambda i: i >= 2 * t)
        own.append(got)
        new.append((2 * t + 2, 2 * t + 2, got))
    if by_shift:

        def useful(i):
            lag = odd_lag if i % 2 else even_lag
            return lag is not None and i + 2 - lag >= 0

        got = upward(after(other[t - 1], *gate), useful)
        other.append(got)
        new.append((even_lag, odd_lag, got))
    elif (to_odd or to_even) and t < len(own):
        got = exchanged(after(own[t], *gate), lambda i: i >= 2 * t and (to_even if i % 2 else to_odd))
        other.append(got)
        new.append((even_lag, odd_lag, got))
    if memory % 2 == 0 and t == memory // 2 and devices - 2 >= memory - 1:
        got = upward(after(other[t - 1], *gate), lambda i: i % 2 == 0 and i + 2 >= memory - 1)
        new.append((memory - 1, None, got))
    return new


def shift_round(memory):
    if memory % 2:
        t = (memory - 1) // 2
    else:
        t = memory // 2 - 1 if lax.axis_size("tm") - 2 < memory - 1 else 0
    return t if t >= 2 else None


def next_in_chain(t, own, memory, gate):
    devices = lax.axis_size("tm")
    if t + 1 >= memory:
        return []
    got = lax.ppermute(after(own[t], *gate), "tm", [(i, i + 1) for i in range(devices - 1)])
    own.append(got)
    return [(t + 1, t + 1, got)]


def bit_reversed(n):
    bits = n.bit_length() - 1
    return [sum(((p >> b) & 1) << (bits - 1 - b) for b in range(bits)) for p in range(n)]


def branch(memory, band, blocks, coef):
    orb = lax.axis_size("orb")
    lag_count = band.shape[2]
    split_band = weighted(band, coef, min(memory, lag_count))
    paired = lax.axis_size("tm") % 2 == 0
    odd = lax.axis_index("tm") % 2 == 1
    power_of_two = orb & (orb - 1) == 0 and orb > 1
    order = jnp.array(bit_reversed(orb) if power_of_two else list(range(orb)), jnp.int32)
    columns = order ^ lax.axis_index("orb").astype(jnp.int32) if power_of_two else order
    count = len(blocks)
    own = [[block] for block in blocks]
    other = [[] for _ in blocks]
    arrived = [[[(0, 0, block)]] for block in blocks]
    totals = [None] * count

    def lag_of(even_lag, odd_lag):
        if even_lag == odd_lag:
            return even_lag
        none = lag_count
        return jnp.where(odd, none if odd_lag is None else odd_lag, none if even_lag is None else even_lag)

    def receive(t, q, gate):
        if paired:
            by_shift = t == shift_round(memory) and count > 2 and q >= (count + 1) // 2
            new = moves(t, own[q], other[q], memory, by_shift, gate)
        else:
            new = next_in_chain(t, own[q], memory, gate)
        if new:
            arrived[q].append(new)
        return bool(new)

    def multiply(r, q, first, tiles, total):
        new = arrived[q][r]
        lags = [lag_of(e, o) for e, o, _ in new]
        return products(split_band, [b for _, _, b in new], lags, columns, total, first, tiles)

    gate = ()
    round_at = 0
    more = True
    while more:
        more = False
        for q in range(count):
            together = tuple(b for _, _, b in arrived[q][-1])
            more = receive(round_at, q, gate + together) or more
            if round_at + 1 < len(arrived[q]):
                totals[q] = multiply(round_at, q, 0, orb, totals[q])
                if round_at > 0 or q == count - 1:
                    gate = (totals[q],)
        round_at += 1

    parts = []
    arriving = None
    for q in range(count):
        r = len(arrived[q]) - 1
        if not power_of_two:
            total = multiply(r, q, 0, orb, totals[q])
            parts.append(lax.psum_scatter(total, "orb", scatter_dimension=0, tiled=True)[0].T)
            continue
        if arriving is not None:
            totals[q] = after(totals[q], arriving)
        elif count > 1:
            totals[q] = after(totals[q], *gate)
        sent = multiply(r, q, orb // 2, orb // 2, totals[q])
        kept = multiply(r, q, 0, orb // 2, totals[q])
        stride = 1
        while True:
            got = lax.ppermute(sent, "orb", [(i, i ^ stride) for i in range(orb)])
            half = kept.shape[0] // 2
            if half == 0:
                break
            sent = kept[half:] + got[half:]
            kept = kept[:half] + got[:half]
            stride *= 2
        arriving = got
        parts.append((kept[0] + got[0]).T)
    return jnp.concatenate(parts, axis=1)


def local(self_energy, history, memory, startup_cut, weight_index, weight_table):
    lag_count = self_energy.shape[2]
    row_total = self_energy.shape[4]
    table_size = weight_table.shape[0]
    lag_ids = jnp.arange(lag_count + 1, dtype=jnp.int32)[:, None]
    row_ids = jnp.arange(row_total, dtype=jnp.int32)[None, :]
    table_ids = jnp.arange(table_size, dtype=jnp.int32)[None, :]
    weights = jnp.sum(
        jnp.where(weight_index[0][:, None] == table_ids, weight_table[None, :], jnp.float32(0.0)),
        axis=1,
    )
    weights = jnp.concatenate([weights, jnp.zeros((1,), jnp.float32)])
    last_lag = memory[0] - 1
    kept_mask = (lag_ids < last_lag) | (lag_ids == last_lag) & (row_ids >= startup_cut[0])
    coef = jnp.where(kept_mask, weights[:, None], jnp.float32(0.0))[:, None, :]
    signs = jnp.array([1.0, -1.0], jnp.float32)[:, None, None]
    _, components, depth, orbitals = history.shape
    width = orbitals // CHUNKS
    blocks = [
        jnp.transpose(history[0, :, :, q * width:(q + 1) * width] * signs, (2, 0, 1)).reshape(width, components * depth)
        for q in range(CHUNKS)
    ]
    least = min(LEAST_MEMORY, lag_count)
    choices = [functools.partial(branch, kept) for kept in range(least, lag_count + 1)]
    collision = lax.switch(jnp.clip(memory[0] - least, 0, len(choices) - 1), choices, self_energy, blocks, coef)
    return collision[None]


def solution(mesh):
    in_specs = (
        P("tm", None, None, "orb", None),
        P("tm", None, "orb", None),
        P(),
        P("tm"),
        P("tm", None),
        P(),
    )
    out_specs = P("tm", "orb", None)
    return jax.shard_map(local, mesh=mesh, in_specs=in_specs, out_specs=out_specs, check_vma=False)
```

```python
import functools

import jax
import jax.numpy as jnp
from jax import lax
from jax.experimental import pallas as pl
from jax.experimental.pallas import tpu as pltpu
from jax.sharding import PartitionSpec as P

CHUNKS = 2
LEAST_MEMORY = 3
STEP = 64
SPAN = 256
VMEM_LIMIT = 20 * 1024 * 1024


def split(value):
    high = value.astype(jnp.bfloat16)
    low = (value - high.astype(jnp.float32)).astype(jnp.bfloat16)
    return high, low


def product_kernel(count, has_total, first, scalars, *refs):
    band_refs = refs[:count]
    coef_refs = refs[count:2 * count]
    block_refs = refs[2 * count:3 * count]
    rest = refs[3 * count:]
    if has_total:
        total_ref, out_ref, left_ref, right_ref = rest
    else:
        out_ref, left_ref, right_ref = rest
    depth = block_refs[0].shape[1]

    width = block_refs[0].shape[0]
    rows = band_refs[0].shape[4]
    band_step = STEP if band_refs[0].shape[3] % STEP == 0 else band_refs[0].shape[3]
    band_steps = band_refs[0].shape[3] // band_step
    block_step = STEP if width % STEP == 0 else width

    @pl.when(pl.program_id(0) == 0)
    def _():
        for q in range(count):

            @pl.loop(0, width // block_step)
            def _(step):
                at = pl.ds(pl.multiple_of(step * block_step, block_step), block_step)
                high, low = split(block_refs[q][at, :])
                for place, part in enumerate((high, low, high)):
                    left_ref[at, pl.ds((3 * q + place) * depth, depth)] = part

    for q in range(count):

        @pl.loop(0, depth // band_step)
        def _(step):
            inner = pl.multiple_of(lax.rem(step, band_steps) * band_step, band_step)
            high, low = split(band_refs[q][0, lax.div(step, band_steps), 0, pl.ds(inner, band_step), :] * coef_refs[q][0])
            for place, part in enumerate((high, high, low)):
                at = pl.multiple_of((3 * q + place) * depth + step * band_step, band_step)
                right_ref[pl.ds(at, band_step), :] = part

    tile = pl.program_id(0)
    across = SPAN if rows % SPAN == 0 else rows

    @pl.loop(0, rows // across)
    def _(step):
        at = pl.ds(pl.multiple_of(step * across, across), across)
        term = jnp.dot(left_ref[...], right_ref[:, at], preferred_element_type=jnp.float32)
        out_ref[tile, :, at] = total_ref[first + tile, :, at] + term if has_total else term


def products(band, coef, blocks, lags, columns, total, first, tiles):
    count = len(blocks)
    _, components, lag_count, depth, row_total = band.shape
    orb = columns.shape[0]
    rows = row_total // orb
    width = blocks[0].shape[0]
    picked = jnp.stack([jnp.asarray(lag, jnp.int32) for lag in lags])
    scalars = jnp.concatenate([jnp.minimum(picked, lag_count - 1), picked, columns[first:first + tiles]])

    def band_map(q, i, s):
        return (0, 0, s[q], 0, s[2 * count + i])

    def coef_map(q, i, s):
        return (s[count + q], 0, s[2 * count + i])

    in_specs = [pl.BlockSpec((1, components, 1, depth, rows), functools.partial(band_map, q)) for q in range(count)]
    in_specs += [pl.BlockSpec((1, 1, rows), functools.partial(coef_map, q)) for q in range(count)]
    in_specs += [pl.BlockSpec(memory_space=pltpu.VMEM) for _ in range(count)]
    operands = [band] * count + [coef] * count + list(blocks)
    if total is not None:
        in_specs.append(pl.BlockSpec(memory_space=pltpu.VMEM))
        operands.append(total)
    in_place = total is not None and tiles == orb
    return pl.pallas_call(
        functools.partial(product_kernel, count, total is not None, first),
        out_shape=jax.ShapeDtypeStruct((tiles, width, rows), jnp.float32),
        grid_spec=pltpu.PrefetchScalarGridSpec(
            num_scalar_prefetch=1,
            grid=(tiles,),
            in_specs=in_specs,
            out_specs=pl.BlockSpec(memory_space=pltpu.VMEM),
            scratch_shapes=[
                pltpu.VMEM((width, 3 * count * components * depth), jnp.bfloat16),
                pltpu.VMEM((3 * count * components * depth, rows), jnp.bfloat16),
            ],
        ),
        input_output_aliases={3 * count + 1: 0} if in_place else {},
        compiler_params=pltpu.CompilerParams(vmem_limit_bytes=VMEM_LIMIT),
        cost_estimate=pl.CostEstimate(flops=1024, bytes_accessed=1024, transcendentals=0),
    )(scalars, *operands)


def upward(value, valid):
    devices = lax.axis_size("tm")
    return lax.ppermute(value, "tm", [(i, i + 2) for i in range(devices - 2) if valid(i)])


def exchanged(value, valid):
    devices = lax.axis_size("tm")
    return lax.ppermute(value, "tm", [(i, i ^ 1) for i in range(devices) if (i ^ 1) < devices and valid(i)])


def after(value, *earlier):
    return lax.optimization_barrier((value,) + earlier)[0]


def moves(t, own, other, memory, by_shift, gate):
    devices = lax.axis_size("tm")
    new = []
    to_odd = 2 * t + 1 < memory
    to_even = 1 <= t and 2 * t - 1 < memory
    even_lag = 2 * t - 1 if to_even else None
    odd_lag = 2 * t + 1 if to_odd else None
    if 2 * (t + 1) < memory:
        got = upward(after(own[t], *gate), lambda i: i >= 2 * t)
        own.append(got)
        new.append((2 * t + 2, 2 * t + 2, got))
    if by_shift:

        def useful(i):
            lag = odd_lag if i % 2 else even_lag
            return lag is not None and i + 2 - lag >= 0

        got = upward(after(other[t - 1], *gate), useful)
        other.append(got)
        new.append((even_lag, odd_lag, got))
    elif (to_odd or to_even) and t < len(own):
        got = exchanged(after(own[t], *gate), lambda i: i >= 2 * t and (to_even if i % 2 else to_odd))
        other.append(got)
        new.append((even_lag, odd_lag, got))
    if memory % 2 == 0 and t == memory // 2 and devices - 2 >= memory - 1:
        got = upward(after(other[t - 1], *gate), lambda i: i % 2 == 0 and i + 2 >= memory - 1)
        new.append((memory - 1, None, got))
    return new


def shift_round(memory):
    if memory % 2:
        t = (memory - 1) // 2
    else:
        t = memory // 2 - 1 if lax.axis_size("tm") - 2 < memory - 1 else 0
    return t if t >= 2 else None


def next_in_chain(t, own, memory, gate):
    devices = lax.axis_size("tm")
    if t + 1 >= memory:
        return []
    got = lax.ppermute(after(own[t], *gate), "tm", [(i, i + 1) for i in range(devices - 1)])
    own.append(got)
    return [(t + 1, t + 1, got)]


def bit_reversed(n):
    bits = n.bit_length() - 1
    return [sum(((p >> b) & 1) << (bits - 1 - b) for b in range(bits)) for p in range(n)]


def branch(memory, band, blocks, coef):
    orb = lax.axis_size("orb")
    lag_count = band.shape[2]
    paired = lax.axis_size("tm") % 2 == 0
    odd = lax.axis_index("tm") % 2 == 1
    power_of_two = orb & (orb - 1) == 0 and orb > 1
    order = jnp.array(bit_reversed(orb) if power_of_two else list(range(orb)), jnp.int32)
    columns = order ^ lax.axis_index("orb").astype(jnp.int32) if power_of_two else order
    count = len(blocks)
    own = [[block] for block in blocks]
    other = [[] for _ in blocks]
    arrived = [[[(0, 0, block)]] for block in blocks]
    totals = [None] * count

    def lag_of(even_lag, odd_lag):
        if even_lag == odd_lag:
            return even_lag
        none = lag_count
        return jnp.where(odd, none if odd_lag is None else odd_lag, none if even_lag is None else even_lag)

    def receive(t, q, gate):
        if paired:
            by_shift = t == shift_round(memory) and count > 2 and q >= (count + 1) // 2
            new = moves(t, own[q], other[q], memory, by_shift, gate)
        else:
            new = next_in_chain(t, own[q], memory, gate)
        if new:
            arrived[q].append(new)
        return bool(new)

    def multiply(r, q, first, tiles, total):
        new = arrived[q][r]
        lags = [lag_of(e, o) for e, o, _ in new]
        return products(band, coef, [b for _, _, b in new], lags, columns, total, first, tiles)

    gate = ()
    round_at = 0
    more = True
    while more:
        more = False
        for q in range(count):
            together = tuple(b for _, _, b in arrived[q][-1])
            more = receive(round_at, q, gate + together) or more
            if round_at + 1 < len(arrived[q]):
                totals[q] = multiply(round_at, q, 0, orb, totals[q])
                if round_at > 0 or q == count - 1:
                    gate = (totals[q],)
        round_at += 1

    parts = []
    arriving = None
    for q in range(count):
        r = len(arrived[q]) - 1
        if not power_of_two:
            total = multiply(r, q, 0, orb, totals[q])
            parts.append(lax.psum_scatter(total, "orb", scatter_dimension=0, tiled=True)[0].T)
            continue
        if arriving is not None:
            totals[q] = after(totals[q], arriving)
        elif count > 1:
            totals[q] = after(totals[q], *gate)
        sent = multiply(r, q, orb // 2, orb // 2, totals[q])
        kept = multiply(r, q, 0, orb // 2, totals[q])
        stride = 1
        while True:
            got = lax.ppermute(sent, "orb", [(i, i ^ stride) for i in range(orb)])
            half = kept.shape[0] // 2
            if half == 0:
                break
            sent = kept[half:] + got[half:]
            kept = kept[:half] + got[:half]
            stride *= 2
        arriving = got
        parts.append((kept[0] + got[0]).T)
    return jnp.concatenate(parts, axis=1)


def local(self_energy, history, memory, startup_cut, weight_index, weight_table):
    lag_count = self_energy.shape[2]
    row_total = self_energy.shape[4]
    table_size = weight_table.shape[0]
    lag_ids = jnp.arange(lag_count + 1, dtype=jnp.int32)[:, None]
    row_ids = jnp.arange(row_total, dtype=jnp.int32)[None, :]
    table_ids = jnp.arange(table_size, dtype=jnp.int32)[None, :]
    weights = jnp.sum(
        jnp.where(weight_index[0][:, None] == table_ids, weight_table[None, :], jnp.float32(0.0)),
        axis=1,
    )
    weights = jnp.concatenate([weights, jnp.zeros((1,), jnp.float32)])
    last_lag = memory[0] - 1
    kept_mask = (lag_ids < last_lag) | (lag_ids == last_lag) & (row_ids >= startup_cut[0])
    coef = jnp.where(kept_mask, weights[:, None], jnp.float32(0.0))[:, None, :]
    signs = jnp.array([1.0, -1.0], jnp.float32)[:, None, None]
    _, components, depth, orbitals = history.shape
    width = orbitals // CHUNKS
    blocks = [
        jnp.transpose(history[0, :, :, q * width:(q + 1) * width] * signs, (2, 0, 1)).reshape(width, components * depth)
        for q in range(CHUNKS)
    ]
    least = min(LEAST_MEMORY, lag_count)
    choices = [functools.partial(branch, kept) for kept in range(least, lag_count + 1)]
    collision = lax.switch(jnp.clip(memory[0] - least, 0, len(choices) - 1), choices, self_energy, blocks, coef)
    return collision[None]


def solution(mesh):
    in_specs = (
        P("tm", None, None, "orb", None),
        P("tm", None, "orb", None),
        P(),
        P("tm"),
        P("tm", None),
        P(),
    )
    out_specs = P("tm", "orb", None)
    return jax.shard_map(local, mesh=mesh, in_specs=in_specs, out_specs=out_specs, check_vma=False)
```

```python
import functools

import jax
import jax.numpy as jnp
from jax import lax
from jax.experimental import pallas as pl
from jax.experimental.pallas import tpu as pltpu
from jax.sharding import PartitionSpec as P

CHUNKS = 2
LEAST_MEMORY = 3
STEP = 128
SPAN = 256
VMEM_LIMIT = 20 * 1024 * 1024


def split(value):
    high = value.astype(jnp.bfloat16)
    low = (value - high.astype(jnp.float32)).astype(jnp.bfloat16)
    return high, low


def product_kernel(count, has_total, first, scalars, *refs):
    band_refs = refs[:count]
    coef_refs = refs[count:2 * count]
    block_refs = refs[2 * count:3 * count]
    rest = refs[3 * count:]
    if has_total:
        total_ref, out_ref, left_ref, right_ref = rest
    else:
        out_ref, left_ref, right_ref = rest
    depth = block_refs[0].shape[1]

    width = block_refs[0].shape[0]
    band_step = STEP if band_refs[0].shape[3] % STEP == 0 else band_refs[0].shape[3]
    band_steps = band_refs[0].shape[3] // band_step
    block_step = STEP if width % STEP == 0 else width

    @pl.when(pl.program_id(0) == 0)
    def _():
        for q in range(count):

            @pl.loop(0, width // block_step)
            def _(step):
                at = pl.ds(pl.multiple_of(step * block_step, block_step), block_step)
                high, low = split(block_refs[q][at, :])
                for place, part in enumerate((high, low, high)):
                    left_ref[at, pl.ds((3 * q + place) * depth, depth)] = part

    for q in range(count):

        @pl.loop(0, depth // band_step)
        def _(step):
            inner = pl.multiple_of(lax.rem(step, band_steps) * band_step, band_step)
            high, low = split(band_refs[q][0, lax.div(step, band_steps), 0, pl.ds(inner, band_step), :] * coef_refs[q][0])
            for place, part in enumerate((high, high, low)):
                at = pl.multiple_of((3 * q + place) * depth + step * band_step, band_step)
                right_ref[pl.ds(at, band_step), :] = part

    tile = pl.program_id(0)
    across = SPAN if width % SPAN == 0 else width

    @pl.loop(0, width // across)
    def _(step):
        at = pl.ds(pl.multiple_of(step * across, across), across)
        term = jnp.dot(left_ref[at, :], right_ref[...], preferred_element_type=jnp.float32)
        out_ref[tile, at, :] = total_ref[first + tile, at, :] + term if has_total else term


def products(band, coef, blocks, lags, columns, total, first, tiles):
    count = len(blocks)
    _, components, lag_count, depth, row_total = band.shape
    orb = columns.shape[0]
    rows = row_total // orb
    width = blocks[0].shape[0]
    picked = jnp.stack([jnp.asarray(lag, jnp.int32) for lag in lags])
    scalars = jnp.concatenate([jnp.minimum(picked, lag_count - 1), picked, columns[first:first + tiles]])

    def band_map(q, i, s):
        return (0, 0, s[q], 0, s[2 * count + i])

    def coef_map(q, i, s):
        return (s[count + q], 0, s[2 * count + i])

    in_specs = [pl.BlockSpec((1, components, 1, depth, rows), functools.partial(band_map, q)) for q in range(count)]
    in_specs += [pl.BlockSpec((1, 1, rows), functools.partial(coef_map, q)) for q in range(count)]
    in_specs += [pl.BlockSpec(memory_space=pltpu.VMEM) for _ in range(count)]
    operands = [band] * count + [coef] * count + list(blocks)
    if total is not None:
        in_specs.append(pl.BlockSpec(memory_space=pltpu.VMEM))
        operands.append(total)
    in_place = total is not None and tiles == orb
    return pl.pallas_call(
        functools.partial(product_kernel, count, total is not None, first),
        out_shape=jax.ShapeDtypeStruct((tiles, width, rows), jnp.float32),
        grid_spec=pltpu.PrefetchScalarGridSpec(
            num_scalar_prefetch=1,
            grid=(tiles,),
            in_specs=in_specs,
            out_specs=pl.BlockSpec(memory_space=pltpu.VMEM),
            scratch_shapes=[
                pltpu.VMEM((width, 3 * count * components * depth), jnp.bfloat16),
                pltpu.VMEM((3 * count * components * depth, rows), jnp.bfloat16),
            ],
        ),
        input_output_aliases={3 * count + 1: 0} if in_place else {},
        compiler_params=pltpu.CompilerParams(vmem_limit_bytes=VMEM_LIMIT),
        cost_estimate=pl.CostEstimate(flops=1024, bytes_accessed=1024, transcendentals=0),
    )(scalars, *operands)


def upward(value, valid):
    devices = lax.axis_size("tm")
    return lax.ppermute(value, "tm", [(i, i + 2) for i in range(devices - 2) if valid(i)])


def exchanged(value, valid):
    devices = lax.axis_size("tm")
    return lax.ppermute(value, "tm", [(i, i ^ 1) for i in range(devices) if (i ^ 1) < devices and valid(i)])


def after(value, *earlier):
    return lax.optimization_barrier((value,) + earlier)[0]


def moves(t, own, other, memory, by_shift, gate):
    devices = lax.axis_size("tm")
    new = []
    to_odd = 2 * t + 1 < memory
    to_even = 1 <= t and 2 * t - 1 < memory
    even_lag = 2 * t - 1 if to_even else None
    odd_lag = 2 * t + 1 if to_odd else None
    if 2 * (t + 1) < memory:
        got = upward(after(own[t], *gate), lambda i: i >= 2 * t)
        own.append(got)
        new.append((2 * t + 2, 2 * t + 2, got))
    if by_shift:

        def useful(i):
            lag = odd_lag if i % 2 else even_lag
            return lag is not None and i + 2 - lag >= 0

        got = upward(after(other[t - 1], *gate), useful)
        other.append(got)
        new.append((even_lag, odd_lag, got))
    elif (to_odd or to_even) and t < len(own):
        got = exchanged(after(own[t], *gate), lambda i: i >= 2 * t and (to_even if i % 2 else to_odd))
        other.append(got)
        new.append((even_lag, odd_lag, got))
    if memory % 2 == 0 and t == memory // 2 and devices - 2 >= memory - 1:
        got = upward(after(other[t - 1], *gate), lambda i: i % 2 == 0 and i + 2 >= memory - 1)
        new.append((memory - 1, None, got))
    return new


def shift_round(memory):
    if memory % 2:
        t = (memory - 1) // 2
    else:
        t = memory // 2 - 1 if lax.axis_size("tm") - 2 < memory - 1 else 0
    return t if t >= 2 else None


def next_in_chain(t, own, memory, gate):
    devices = lax.axis_size("tm")
    if t + 1 >= memory:
        return []
    got = lax.ppermute(after(own[t], *gate), "tm", [(i, i + 1) for i in range(devices - 1)])
    own.append(got)
    return [(t + 1, t + 1, got)]


def bit_reversed(n):
    bits = n.bit_length() - 1
    return [sum(((p >> b) & 1) << (bits - 1 - b) for b in range(bits)) for p in range(n)]


def branch(memory, band, blocks, coef):
    orb = lax.axis_size("orb")
    lag_count = band.shape[2]
    paired = lax.axis_size("tm") % 2 == 0
    odd = lax.axis_index("tm") % 2 == 1
    power_of_two = orb & (orb - 1) == 0 and orb > 1
    order = jnp.array(bit_reversed(orb) if power_of_two else list(range(orb)), jnp.int32)
    columns = order ^ lax.axis_index("orb").astype(jnp.int32) if power_of_two else order
    count = len(blocks)
    own = [[block] for block in blocks]
    other = [[] for _ in blocks]
    arrived = [[[(0, 0, block)]] for block in blocks]
    totals = [None] * count

    def lag_of(even_lag, odd_lag):
        if even_lag == odd_lag:
            return even_lag
        none = lag_count
        return jnp.where(odd, none if odd_lag is None else odd_lag, none if even_lag is None else even_lag)

    def receive(t, q, gate):
        if paired:
            by_shift = t == shift_round(memory) and count > 2 and q >= (count + 1) // 2
            new = moves(t, own[q], other[q], memory, by_shift, gate)
        else:
            new = next_in_chain(t, own[q], memory, gate)
        if new:
            arrived[q].append(new)
        return bool(new)

    def multiply(r, q, first, tiles, total):
        new = arrived[q][r]
        lags = [lag_of(e, o) for e, o, _ in new]
        return products(band, coef, [b for _, _, b in new], lags, columns, total, first, tiles)

    gate = ()
    round_at = 0
    more = True
    while more:
        more = False
        for q in range(count):
            together = tuple(b for _, _, b in arrived[q][-1])
            more = receive(round_at, q, gate + together) or more
            if round_at + 1 < len(arrived[q]):
                totals[q] = multiply(round_at, q, 0, orb, totals[q])
                if round_at > 0 or q == count - 1:
                    gate = (totals[q],)
        round_at += 1

    parts = []
    arriving = None
    for q in range(count):
        r = len(arrived[q]) - 1
        if not power_of_two:
            total = multiply(r, q, 0, orb, totals[q])
            parts.append(lax.psum_scatter(total, "orb", scatter_dimension=0, tiled=True)[0].T)
            continue
        if arriving is not None:
            totals[q] = after(totals[q], arriving)
        elif count > 1:
            totals[q] = after(totals[q], *gate)
        sent = multiply(r, q, orb // 2, orb // 2, totals[q])
        kept = multiply(r, q, 0, orb // 2, totals[q])
        stride = 1
        while True:
            got = lax.ppermute(sent, "orb", [(i, i ^ stride) for i in range(orb)])
            half = kept.shape[0] // 2
            if half == 0:
                break
            sent = kept[half:] + got[half:]
            kept = kept[:half] + got[:half]
            stride *= 2
        arriving = got
        parts.append((kept[0] + got[0]).T)
    return jnp.concatenate(parts, axis=1)


def local(self_energy, history, memory, startup_cut, weight_index, weight_table):
    lag_count = self_energy.shape[2]
    row_total = self_energy.shape[4]
    table_size = weight_table.shape[0]
    lag_ids = jnp.arange(lag_count + 1, dtype=jnp.int32)[:, None]
    row_ids = jnp.arange(row_total, dtype=jnp.int32)[None, :]
    table_ids = jnp.arange(table_size, dtype=jnp.int32)[None, :]
    weights = jnp.sum(
        jnp.where(weight_index[0][:, None] == table_ids, weight_table[None, :], jnp.float32(0.0)),
        axis=1,
    )
    weights = jnp.concatenate([weights, jnp.zeros((1,), jnp.float32)])
    last_lag = memory[0] - 1
    kept_mask = (lag_ids < last_lag) | (lag_ids == last_lag) & (row_ids >= startup_cut[0])
    coef = jnp.where(kept_mask, weights[:, None], jnp.float32(0.0))[:, None, :]
    signs = jnp.array([1.0, -1.0], jnp.float32)[:, None, None]
    _, components, depth, orbitals = history.shape
    width = orbitals // CHUNKS
    blocks = [
        jnp.transpose(history[0, :, :, q * width:(q + 1) * width] * signs, (2, 0, 1)).reshape(width, components * depth)
        for q in range(CHUNKS)
    ]
    least = min(LEAST_MEMORY, lag_count)
    choices = [functools.partial(branch, kept) for kept in range(least, lag_count + 1)]
    collision = lax.switch(jnp.clip(memory[0] - least, 0, len(choices) - 1), choices, self_energy, blocks, coef)
    return collision[None]


def solution(mesh):
    in_specs = (
        P("tm", None, None, "orb", None),
        P("tm", None, "orb", None),
        P(),
        P("tm"),
        P("tm", None),
        P(),
    )
    out_specs = P("tm", "orb", None)
    return jax.shard_map(local, mesh=mesh, in_specs=in_specs, out_specs=out_specs, check_vma=False)
```

```python
import functools

import jax
import jax.numpy as jnp
from jax import lax
from jax.experimental import pallas as pl
from jax.experimental.pallas import tpu as pltpu
from jax.sharding import PartitionSpec as P

CHUNKS = 2
LEAST_MEMORY = 3
STEP = 128
VMEM_LIMIT = 20 * 1024 * 1024


def split(value):
    high = value.astype(jnp.bfloat16)
    low = (value - high.astype(jnp.float32)).astype(jnp.bfloat16)
    return high, low


def product_kernel(count, has_total, first, scalars, *refs):
    band_refs = refs[:count]
    coef_refs = refs[count:2 * count]
    block_refs = refs[2 * count:3 * count]
    rest = refs[3 * count:]
    if has_total:
        total_ref, out_ref, left_ref, right_ref = rest
    else:
        out_ref, left_ref, right_ref = rest
    depth = block_refs[0].shape[1]

    width = block_refs[0].shape[0]
    band_step = STEP if band_refs[0].shape[3] % STEP == 0 else band_refs[0].shape[3]
    band_steps = band_refs[0].shape[3] // band_step
    block_step = STEP if width % STEP == 0 else width

    width = block_refs[0].shape[0]
    inner = band_refs[0].shape[3]
    band_step = STEP if inner % STEP == 0 else inner
    block_step = STEP if width % STEP == 0 else width

    @pl.when(pl.program_id(0) == 0)
    def _():
        for q in range(count):

            @pl.loop(0, width // block_step)
            def _(step):
                at = pl.ds(pl.multiple_of(step * block_step, block_step), block_step)
                left_ref[2 * q, at, :], left_ref[2 * q + 1, at, :] = split(block_refs[q][at, :])

    for q in range(count):

        @pl.loop(0, depth // band_step)
        def _(step):
            c = lax.div(step * band_step, inner)
            row = pl.multiple_of(step * band_step - c * inner, band_step)
            at = pl.ds(pl.multiple_of(step * band_step, band_step), band_step)
            band = band_refs[q][0, c, 0, pl.ds(row, band_step), :] * coef_refs[q][0]
            right_ref[2 * q, at, :], right_ref[2 * q + 1, at, :] = split(band)

    tile = pl.program_id(0)
    out_ref[tile] = total_ref[first + tile] if has_total else jnp.zeros(out_ref.shape[1:], jnp.float32)

    @pl.loop(0, 3 * count)
    def _(term):
        q = lax.div(term, 3)
        kind = term - 3 * q
        left = left_ref[2 * q + jnp.where(kind == 1, 1, 0)]
        right = right_ref[2 * q + jnp.where(kind == 2, 1, 0)]
        out_ref[tile] += jnp.dot(left, right, preferred_element_type=jnp.float32)


def products(band, coef, blocks, lags, columns, total, first, tiles):
    count = len(blocks)
    _, components, lag_count, depth, row_total = band.shape
    orb = columns.shape[0]
    rows = row_total // orb
    width = blocks[0].shape[0]
    picked = jnp.stack([jnp.asarray(lag, jnp.int32) for lag in lags])
    scalars = jnp.concatenate([jnp.minimum(picked, lag_count - 1), picked, columns[first:first + tiles]])

    def band_map(q, i, s):
        return (0, 0, s[q], 0, s[2 * count + i])

    def coef_map(q, i, s):
        return (s[count + q], 0, s[2 * count + i])

    in_specs = [pl.BlockSpec((1, components, 1, depth, rows), functools.partial(band_map, q)) for q in range(count)]
    in_specs += [pl.BlockSpec((1, 1, rows), functools.partial(coef_map, q)) for q in range(count)]
    in_specs += [pl.BlockSpec(memory_space=pltpu.VMEM) for _ in range(count)]
    operands = [band] * count + [coef] * count + list(blocks)
    if total is not None:
        in_specs.append(pl.BlockSpec(memory_space=pltpu.VMEM))
        operands.append(total)
    in_place = total is not None and tiles == orb
    return pl.pallas_call(
        functools.partial(product_kernel, count, total is not None, first),
        out_shape=jax.ShapeDtypeStruct((tiles, width, rows), jnp.float32),
        grid_spec=pltpu.PrefetchScalarGridSpec(
            num_scalar_prefetch=1,
            grid=(tiles,),
            in_specs=in_specs,
            out_specs=pl.BlockSpec(memory_space=pltpu.VMEM),
            scratch_shapes=[
                pltpu.VMEM((2 * count, width, components * depth), jnp.bfloat16),
                pltpu.VMEM((2 * count, components * depth, rows), jnp.bfloat16),
            ],
        ),
        input_output_aliases={3 * count + 1: 0} if in_place else {},
        compiler_params=pltpu.CompilerParams(vmem_limit_bytes=VMEM_LIMIT),
        cost_estimate=pl.CostEstimate(flops=1024, bytes_accessed=1024, transcendentals=0),
    )(scalars, *operands)


def upward(value, valid):
    devices = lax.axis_size("tm")
    return lax.ppermute(value, "tm", [(i, i + 2) for i in range(devices - 2) if valid(i)])


def exchanged(value, valid):
    devices = lax.axis_size("tm")
    return lax.ppermute(value, "tm", [(i, i ^ 1) for i in range(devices) if (i ^ 1) < devices and valid(i)])


def after(value, *earlier):
    return lax.optimization_barrier((value,) + earlier)[0]


def moves(t, own, other, memory, by_shift, gate):
    devices = lax.axis_size("tm")
    new = []
    to_odd = 2 * t + 1 < memory
    to_even = 1 <= t and 2 * t - 1 < memory
    even_lag = 2 * t - 1 if to_even else None
    odd_lag = 2 * t + 1 if to_odd else None
    if 2 * (t + 1) < memory:
        got = upward(after(own[t], *gate), lambda i: i >= 2 * t)
        own.append(got)
        new.append((2 * t + 2, 2 * t + 2, got))
    if by_shift:

        def useful(i):
            lag = odd_lag if i % 2 else even_lag
            return lag is not None and i + 2 - lag >= 0

        got = upward(after(other[t - 1], *gate), useful)
        other.append(got)
        new.append((even_lag, odd_lag, got))
    elif (to_odd or to_even) and t < len(own):
        got = exchanged(after(own[t], *gate), lambda i: i >= 2 * t and (to_even if i % 2 else to_odd))
        other.append(got)
        new.append((even_lag, odd_lag, got))
    if memory % 2 == 0 and t == memory // 2 and devices - 2 >= memory - 1:
        got = upward(after(other[t - 1], *gate), lambda i: i % 2 == 0 and i + 2 >= memory - 1)
        new.append((memory - 1, None, got))
    return new


def shift_round(memory):
    if memory % 2:
        t = (memory - 1) // 2
    else:
        t = memory // 2 - 1 if lax.axis_size("tm") - 2 < memory - 1 else 0
    return t if t >= 2 else None


def next_in_chain(t, own, memory, gate):
    devices = lax.axis_size("tm")
    if t + 1 >= memory:
        return []
    got = lax.ppermute(after(own[t], *gate), "tm", [(i, i + 1) for i in range(devices - 1)])
    own.append(got)
    return [(t + 1, t + 1, got)]


def bit_reversed(n):
    bits = n.bit_length() - 1
    return [sum(((p >> b) & 1) << (bits - 1 - b) for b in range(bits)) for p in range(n)]


def branch(memory, band, blocks, coef):
    orb = lax.axis_size("orb")
    lag_count = band.shape[2]
    paired = lax.axis_size("tm") % 2 == 0
    odd = lax.axis_index("tm") % 2 == 1
    power_of_two = orb & (orb - 1) == 0 and orb > 1
    order = jnp.array(bit_reversed(orb) if power_of_two else list(range(orb)), jnp.int32)
    columns = order ^ lax.axis_index("orb").astype(jnp.int32) if power_of_two else order
    count = len(blocks)
    own = [[block] for block in blocks]
    other = [[] for _ in blocks]
    arrived = [[[(0, 0, block)]] for block in blocks]
    totals = [None] * count

    def lag_of(even_lag, odd_lag):
        if even_lag == odd_lag:
            return even_lag
        none = lag_count
        return jnp.where(odd, none if odd_lag is None else odd_lag, none if even_lag is None else even_lag)

    def receive(t, q, gate):
        if paired:
            by_shift = t == shift_round(memory) and count > 2 and q >= (count + 1) // 2
            new = moves(t, own[q], other[q], memory, by_shift, gate)
        else:
            new = next_in_chain(t, own[q], memory, gate)
        if new:
            arrived[q].append(new)
        return bool(new)

    def multiply(r, q, first, tiles, total):
        new = arrived[q][r]
        lags = [lag_of(e, o) for e, o, _ in new]
        return products(band, coef, [b for _, _, b in new], lags, columns, total, first, tiles)

    gate = ()
    round_at = 0
    more = True
    while more:
        more = False
        for q in range(count):
            together = tuple(b for _, _, b in arrived[q][-1])
            more = receive(round_at, q, gate + together) or more
            if round_at + 1 < len(arrived[q]):
                totals[q] = multiply(round_at, q, 0, orb, totals[q])
                if round_at > 0 or q == count - 1:
                    gate = (totals[q],)
        round_at += 1

    parts = []
    arriving = None
    for q in range(count):
        r = len(arrived[q]) - 1
        if not power_of_two:
            total = multiply(r, q, 0, orb, totals[q])
            parts.append(lax.psum_scatter(total, "orb", scatter_dimension=0, tiled=True)[0].T)
            continue
        if arriving is not None:
            totals[q] = after(totals[q], arriving)
        elif count > 1:
            totals[q] = after(totals[q], *gate)
        sent = multiply(r, q, orb // 2, orb // 2, totals[q])
        kept = multiply(r, q, 0, orb // 2, totals[q])
        stride = 1
        while True:
            got = lax.ppermute(sent, "orb", [(i, i ^ stride) for i in range(orb)])
            half = kept.shape[0] // 2
            if half == 0:
                break
            sent = kept[half:] + got[half:]
            kept = kept[:half] + got[:half]
            stride *= 2
        arriving = got
        parts.append((kept[0] + got[0]).T)
    return jnp.concatenate(parts, axis=1)


def local(self_energy, history, memory, startup_cut, weight_index, weight_table):
    lag_count = self_energy.shape[2]
    row_total = self_energy.shape[4]
    table_size = weight_table.shape[0]
    lag_ids = jnp.arange(lag_count + 1, dtype=jnp.int32)[:, None]
    row_ids = jnp.arange(row_total, dtype=jnp.int32)[None, :]
    table_ids = jnp.arange(table_size, dtype=jnp.int32)[None, :]
    weights = jnp.sum(
        jnp.where(weight_index[0][:, None] == table_ids, weight_table[None, :], jnp.float32(0.0)),
        axis=1,
    )
    weights = jnp.concatenate([weights, jnp.zeros((1,), jnp.float32)])
    last_lag = memory[0] - 1
    kept_mask = (lag_ids < last_lag) | (lag_ids == last_lag) & (row_ids >= startup_cut[0])
    coef = jnp.where(kept_mask, weights[:, None], jnp.float32(0.0))[:, None, :]
    signs = jnp.array([1.0, -1.0], jnp.float32)[:, None, None]
    _, components, depth, orbitals = history.shape
    width = orbitals // CHUNKS
    blocks = [
        jnp.transpose(history[0, :, :, q * width:(q + 1) * width] * signs, (2, 0, 1)).reshape(width, components * depth)
        for q in range(CHUNKS)
    ]
    least = min(LEAST_MEMORY, lag_count)
    choices = [functools.partial(branch, kept) for kept in range(least, lag_count + 1)]
    collision = lax.switch(jnp.clip(memory[0] - least, 0, len(choices) - 1), choices, self_energy, blocks, coef)
    return collision[None]


def solution(mesh):
    in_specs = (
        P("tm", None, None, "orb", None),
        P("tm", None, "orb", None),
        P(),
        P("tm"),
        P("tm", None),
        P(),
    )
    out_specs = P("tm", "orb", None)
    return jax.shard_map(local, mesh=mesh, in_specs=in_specs, out_specs=out_specs, check_vma=False)
```

```python
import functools

import jax
import jax.numpy as jnp
from jax import lax
from jax.experimental import pallas as pl
from jax.experimental.pallas import tpu as pltpu
from jax.sharding import PartitionSpec as P

CHUNKS = 2
LEAST_MEMORY = 3
MARKER_COST = 60 * 10**9
STEP = 128
SPAN = 256
VMEM_LIMIT = 20 * 1024 * 1024


def split(value):
    high = value.astype(jnp.bfloat16)
    low = (value - high.astype(jnp.float32)).astype(jnp.bfloat16)
    return high, low


def product_kernel(count, has_total, first, scalars, *refs):
    band_refs = refs[:count]
    coef_refs = refs[count:2 * count]
    block_refs = refs[2 * count:3 * count]
    rest = refs[3 * count:]
    if has_total:
        total_ref, out_ref, left_ref, right_ref = rest
    else:
        out_ref, left_ref, right_ref = rest
    depth = block_refs[0].shape[1]

    width = block_refs[0].shape[0]
    band_step = STEP if band_refs[0].shape[3] % STEP == 0 else band_refs[0].shape[3]
    band_steps = band_refs[0].shape[3] // band_step
    block_step = STEP if width % STEP == 0 else width

    @pl.when(pl.program_id(0) == 0)
    def _():
        for q in range(count):

            @pl.loop(0, width // block_step)
            def _(step):
                at = pl.ds(pl.multiple_of(step * block_step, block_step), block_step)
                high, low = split(block_refs[q][at, :])
                for place, part in enumerate((high, low, high)):
                    left_ref[at, pl.ds((3 * q + place) * depth, depth)] = part

    for q in range(count):

        @pl.loop(0, depth // band_step)
        def _(step):
            inner = pl.multiple_of(lax.rem(step, band_steps) * band_step, band_step)
            high, low = split(band_refs[q][0, lax.div(step, band_steps), 0, pl.ds(inner, band_step), :] * coef_refs[q][0])
            for place, part in enumerate((high, high, low)):
                at = pl.multiple_of((3 * q + place) * depth + step * band_step, band_step)
                right_ref[pl.ds(at, band_step), :] = part

    tile = pl.program_id(0)
    across = SPAN if width % SPAN == 0 else width

    @pl.loop(0, width // across)
    def _(step):
        at = pl.ds(pl.multiple_of(step * across, across), across)
        term = jnp.dot(left_ref[at, :], right_ref[...], preferred_element_type=jnp.float32)
        out_ref[tile, at, :] = total_ref[first + tile, at, :] + term if has_total else term


def products(band, coef, blocks, lags, columns, total, first, tiles):
    count = len(blocks)
    _, components, lag_count, depth, row_total = band.shape
    orb = columns.shape[0]
    rows = row_total // orb
    width = blocks[0].shape[0]
    picked = jnp.stack([jnp.asarray(lag, jnp.int32) for lag in lags])
    scalars = jnp.concatenate([jnp.minimum(picked, lag_count - 1), picked, columns[first:first + tiles]])

    def band_map(q, i, s):
        return (0, 0, s[q], 0, s[2 * count + i])

    def coef_map(q, i, s):
        return (s[count + q], 0, s[2 * count + i])

    in_specs = [pl.BlockSpec((1, components, 1, depth, rows), functools.partial(band_map, q)) for q in range(count)]
    in_specs += [pl.BlockSpec((1, 1, rows), functools.partial(coef_map, q)) for q in range(count)]
    in_specs += [pl.BlockSpec(memory_space=pltpu.VMEM) for _ in range(count)]
    operands = [band] * count + [coef] * count + list(blocks)
    if total is not None:
        in_specs.append(pl.BlockSpec(memory_space=pltpu.VMEM))
        operands.append(total)
    in_place = total is not None and tiles == orb
    return pl.pallas_call(
        functools.partial(product_kernel, count, total is not None, first),
        out_shape=jax.ShapeDtypeStruct((tiles, width, rows), jnp.float32),
        grid_spec=pltpu.PrefetchScalarGridSpec(
            num_scalar_prefetch=1,
            grid=(tiles,),
            in_specs=in_specs,
            out_specs=pl.BlockSpec(memory_space=pltpu.VMEM),
            scratch_shapes=[
                pltpu.VMEM((width, 3 * count * components * depth), jnp.bfloat16),
                pltpu.VMEM((3 * count * components * depth, rows), jnp.bfloat16),
            ],
        ),
        input_output_aliases={3 * count + 1: 0} if in_place else {},
        compiler_params=pltpu.CompilerParams(vmem_limit_bytes=VMEM_LIMIT),
        cost_estimate=pl.CostEstimate(flops=1024, bytes_accessed=1024, transcendentals=0),
    )(scalars, *operands)


def upward(value, valid):
    devices = lax.axis_size("tm")
    return lax.ppermute(value, "tm", [(i, i + 2) for i in range(devices - 2) if valid(i)])


def exchanged(value, valid):
    devices = lax.axis_size("tm")
    return lax.ppermute(value, "tm", [(i, i ^ 1) for i in range(devices) if (i ^ 1) < devices and valid(i)])


def after(value, *earlier):
    return lax.optimization_barrier((value,) + earlier)[0]


def moves(t, own, other, memory, by_shift, gate):
    devices = lax.axis_size("tm")
    new = []
    to_odd = 2 * t + 1 < memory
    to_even = 1 <= t and 2 * t - 1 < memory
    even_lag = 2 * t - 1 if to_even else None
    odd_lag = 2 * t + 1 if to_odd else None
    if 2 * (t + 1) < memory:
        got = upward(after(own[t], *gate), lambda i: i >= 2 * t)
        own.append(got)
        new.append((2 * t + 2, 2 * t + 2, got))
    if by_shift:

        def useful(i):
            lag = odd_lag if i % 2 else even_lag
            return lag is not None and i + 2 - lag >= 0

        got = upward(after(other[t - 1], *gate), useful)
        other.append(got)
        new.append((even_lag, odd_lag, got))
    elif (to_odd or to_even) and t < len(own):
        got = exchanged(after(own[t], *gate), lambda i: i >= 2 * t and (to_even if i % 2 else to_odd))
        other.append(got)
        new.append((even_lag, odd_lag, got))
    if memory % 2 == 0 and t == memory // 2 and devices - 2 >= memory - 1:
        got = upward(after(other[t - 1], *gate), lambda i: i % 2 == 0 and i + 2 >= memory - 1)
        new.append((memory - 1, None, got))
    return new


def shift_round(memory):
    if memory % 2:
        t = (memory - 1) // 2
    else:
        t = memory // 2 - 1 if lax.axis_size("tm") - 2 < memory - 1 else 0
    return t if t >= 2 else None


def next_in_chain(t, own, memory, gate):
    devices = lax.axis_size("tm")
    if t + 1 >= memory:
        return []
    got = lax.ppermute(after(own[t], *gate), "tm", [(i, i + 1) for i in range(devices - 1)])
    own.append(got)
    return [(t + 1, t + 1, got)]


def marker_kernel(value_ref, out_ref):
    out_ref[...] = jnp.zeros_like(out_ref)


def marker(value):
    zeros = pl.pallas_call(
        marker_kernel,
        out_shape=jax.ShapeDtypeStruct((8, 128), jnp.float32),
        in_specs=[pl.BlockSpec(memory_space=pl.ANY)],
        out_specs=pl.BlockSpec(memory_space=pltpu.VMEM),
        compiler_params=pltpu.CompilerParams(vmem_limit_bytes=VMEM_LIMIT),
        cost_estimate=pl.CostEstimate(flops=MARKER_COST, bytes_accessed=1024, transcendentals=0),
    )(value)
    return zeros[0, 0]


def bit_reversed(n):
    bits = n.bit_length() - 1
    return [sum(((p >> b) & 1) << (bits - 1 - b) for b in range(bits)) for p in range(n)]


def branch(memory, band, blocks, coef):
    orb = lax.axis_size("orb")
    lag_count = band.shape[2]
    paired = lax.axis_size("tm") % 2 == 0
    odd = lax.axis_index("tm") % 2 == 1
    power_of_two = orb & (orb - 1) == 0 and orb > 1
    order = jnp.array(bit_reversed(orb) if power_of_two else list(range(orb)), jnp.int32)
    columns = order ^ lax.axis_index("orb").astype(jnp.int32) if power_of_two else order
    count = len(blocks)
    own = [[block] for block in blocks]
    other = [[] for _ in blocks]
    arrived = [[[(0, 0, block)]] for block in blocks]
    totals = [None] * count

    def lag_of(even_lag, odd_lag):
        if even_lag == odd_lag:
            return even_lag
        none = lag_count
        return jnp.where(odd, none if odd_lag is None else odd_lag, none if even_lag is None else even_lag)

    def receive(t, q, gate):
        if paired:
            by_shift = t == shift_round(memory) and count > 2 and q >= (count + 1) // 2
            new = moves(t, own[q], other[q], memory, by_shift, gate)
        else:
            new = next_in_chain(t, own[q], memory, gate)
        if new:
            arrived[q].append(new)
        return bool(new)

    def multiply(r, q, first, tiles, total):
        new = arrived[q][r]
        lags = [lag_of(e, o) for e, o, _ in new]
        return products(band, coef, [b for _, _, b in new], lags, columns, total, first, tiles)

    gate = ()
    round_at = 0
    more = True
    while more:
        more = False
        for q in range(count):
            together = tuple(b for _, _, b in arrived[q][-1])
            more = receive(round_at, q, gate + together) or more
            if round_at + 1 < len(arrived[q]):
                totals[q] = multiply(round_at, q, 0, orb, totals[q])
                if round_at > 0 or q == count - 1:
                    gate = (totals[q],)
        round_at += 1

    parts = []
    sending = arriving = None
    for q in range(count):
        r = len(arrived[q]) - 1
        if not power_of_two:
            total = multiply(r, q, 0, orb, totals[q])
            parts.append(lax.psum_scatter(total, "orb", scatter_dimension=0, tiled=True)[0].T)
            continue
        if sending is not None:
            totals[q] = after(totals[q], sending)
        elif count > 1:
            totals[q] = after(totals[q], *gate)
        sent = multiply(r, q, orb // 2, orb // 2, totals[q])
        kept = multiply(r, q, 0, orb // 2, totals[q])
        stride = 1
        while True:
            sending = sent
            got = lax.ppermute(sent, "orb", [(i, i ^ stride) for i in range(orb)])
            half = kept.shape[0] // 2
            if half == 0:
                break
            sent = kept[half:] + got[half:]
            kept = kept[:half] + got[:half]
            stride *= 2
            if arriving is not None and stride == orb // 2:
                sent = sent + marker(arriving)
        arriving = got
        parts.append((kept[0] + got[0]).T)
    return jnp.concatenate(parts, axis=1)


def local(self_energy, history, memory, startup_cut, weight_index, weight_table):
    lag_count = self_energy.shape[2]
    row_total = self_energy.shape[4]
    table_size = weight_table.shape[0]
    lag_ids = jnp.arange(lag_count + 1, dtype=jnp.int32)[:, None]
    row_ids = jnp.arange(row_total, dtype=jnp.int32)[None, :]
    table_ids = jnp.arange(table_size, dtype=jnp.int32)[None, :]
    weights = jnp.sum(
        jnp.where(weight_index[0][:, None] == table_ids, weight_table[None, :], jnp.float32(0.0)),
        axis=1,
    )
    weights = jnp.concatenate([weights, jnp.zeros((1,), jnp.float32)])
    last_lag = memory[0] - 1
    kept_mask = (lag_ids < last_lag) | (lag_ids == last_lag) & (row_ids >= startup_cut[0])
    coef = jnp.where(kept_mask, weights[:, None], jnp.float32(0.0))[:, None, :]
    signs = jnp.array([1.0, -1.0], jnp.float32)[:, None, None]
    _, components, depth, orbitals = history.shape
    width = orbitals // CHUNKS
    blocks = [
        jnp.transpose(history[0, :, :, q * width:(q + 1) * width] * signs, (2, 0, 1)).reshape(width, components * depth)
        for q in range(CHUNKS)
    ]
    least = min(LEAST_MEMORY, lag_count)
    choices = [functools.partial(branch, kept) for kept in range(least, lag_count + 1)]
    collision = lax.switch(jnp.clip(memory[0] - least, 0, len(choices) - 1), choices, self_energy, blocks, coef)
    return collision[None]


def solution(mesh):
    in_specs = (
        P("tm", None, None, "orb", None),
        P("tm", None, "orb", None),
        P(),
        P("tm"),
        P("tm", None),
        P(),
    )
    out_specs = P("tm", "orb", None)
    return jax.shard_map(local, mesh=mesh, in_specs=in_specs, out_specs=out_specs, check_vma=False)
```

```python
import functools

import jax
import jax.numpy as jnp
from jax import lax
from jax.experimental import pallas as pl
from jax.experimental.pallas import tpu as pltpu
from jax.sharding import PartitionSpec as P

CHUNKS = 2
LEAST_MEMORY = 3
MARKER_COST = 60 * 10**9
STEP = 128
SPAN = 256
VMEM_LIMIT = 20 * 1024 * 1024


def split(value):
    high = value.astype(jnp.bfloat16)
    low = (value - high.astype(jnp.float32)).astype(jnp.bfloat16)
    return high, low


def product_kernel(count, has_total, first, scalars, *refs):
    band_refs = refs[:count]
    coef_refs = refs[count:2 * count]
    block_refs = refs[2 * count:3 * count]
    rest = refs[3 * count:]
    if has_total:
        total_ref, out_ref, left_ref, right_ref = rest
    else:
        out_ref, left_ref, right_ref = rest
    depth = block_refs[0].shape[1]

    width = block_refs[0].shape[0]
    band_step = STEP if band_refs[0].shape[3] % STEP == 0 else band_refs[0].shape[3]
    band_steps = band_refs[0].shape[3] // band_step
    block_step = STEP if width % STEP == 0 else width

    @pl.when(pl.program_id(0) == 0)
    def _():
        for q in range(count):

            @pl.loop(0, width // block_step)
            def _(step):
                at = pl.ds(pl.multiple_of(step * block_step, block_step), block_step)
                high, low = split(block_refs[q][at, :])
                for place, part in enumerate((high, low, high)):
                    left_ref[at, pl.ds((3 * q + place) * depth, depth)] = part

    for q in range(count):

        @pl.loop(0, depth // band_step)
        def _(step):
            inner = pl.multiple_of(lax.rem(step, band_steps) * band_step, band_step)
            high, low = split(band_refs[q][0, lax.div(step, band_steps), 0, pl.ds(inner, band_step), :] * coef_refs[q][0])
            for place, part in enumerate((high, high, low)):
                at = pl.multiple_of((3 * q + place) * depth + step * band_step, band_step)
                right_ref[pl.ds(at, band_step), :] = part

    tile = pl.program_id(0)
    across = SPAN if width % SPAN == 0 else width

    @pl.loop(0, width // across)
    def _(step):
        at = pl.ds(pl.multiple_of(step * across, across), across)
        term = jnp.dot(left_ref[at, :], right_ref[...], preferred_element_type=jnp.float32)
        out_ref[tile, at, :] = total_ref[first + tile, at, :] + term if has_total else term


def products(band, coef, blocks, lags, columns, total, first, tiles):
    count = len(blocks)
    _, components, lag_count, depth, row_total = band.shape
    orb = columns.shape[0]
    rows = row_total // orb
    width = blocks[0].shape[0]
    picked = jnp.stack([jnp.asarray(lag, jnp.int32) for lag in lags])
    scalars = jnp.concatenate([jnp.minimum(picked, lag_count - 1), picked, columns[first:first + tiles]])

    def band_map(q, i, s):
        return (0, 0, s[q], 0, s[2 * count + i])

    def coef_map(q, i, s):
        return (s[count + q], 0, s[2 * count + i])

    in_specs = [pl.BlockSpec((1, components, 1, depth, rows), functools.partial(band_map, q)) for q in range(count)]
    in_specs += [pl.BlockSpec((1, 1, rows), functools.partial(coef_map, q)) for q in range(count)]
    in_specs += [pl.BlockSpec(memory_space=pltpu.VMEM) for _ in range(count)]
    operands = [band] * count + [coef] * count + list(blocks)
    if total is not None:
        in_specs.append(pl.BlockSpec(memory_space=pltpu.VMEM))
        operands.append(total)
    in_place = total is not None and tiles == orb
    return pl.pallas_call(
        functools.partial(product_kernel, count, total is not None, first),
        out_shape=jax.ShapeDtypeStruct((tiles, width, rows), jnp.float32),
        grid_spec=pltpu.PrefetchScalarGridSpec(
            num_scalar_prefetch=1,
            grid=(tiles,),
            in_specs=in_specs,
            out_specs=pl.BlockSpec(memory_space=pltpu.VMEM),
            scratch_shapes=[
                pltpu.VMEM((width, 3 * count * components * depth), jnp.bfloat16),
                pltpu.VMEM((3 * count * components * depth, rows), jnp.bfloat16),
            ],
        ),
        input_output_aliases={3 * count + 1: 0} if in_place else {},
        compiler_params=pltpu.CompilerParams(vmem_limit_bytes=VMEM_LIMIT),
        cost_estimate=pl.CostEstimate(flops=1024, bytes_accessed=1024, transcendentals=0),
    )(scalars, *operands)


def upward(value, valid):
    devices = lax.axis_size("tm")
    return lax.ppermute(value, "tm", [(i, i + 2) for i in range(devices - 2) if valid(i)])


def exchanged(value, valid):
    devices = lax.axis_size("tm")
    return lax.ppermute(value, "tm", [(i, i ^ 1) for i in range(devices) if (i ^ 1) < devices and valid(i)])


def after(value, *earlier):
    return lax.optimization_barrier((value,) + earlier)[0]


def moves(t, own, other, memory, by_shift, gate):
    devices = lax.axis_size("tm")
    new = []
    to_odd = 2 * t + 1 < memory
    to_even = 1 <= t and 2 * t - 1 < memory
    even_lag = 2 * t - 1 if to_even else None
    odd_lag = 2 * t + 1 if to_odd else None
    if 2 * (t + 1) < memory:
        got = upward(after(own[t], *gate), lambda i: i >= 2 * t)
        own.append(got)
        new.append((2 * t + 2, 2 * t + 2, got))
    if by_shift:

        def useful(i):
            lag = odd_lag if i % 2 else even_lag
            return lag is not None and i + 2 - lag >= 0

        got = upward(after(other[t - 1], *gate), useful)
        other.append(got)
        new.append((even_lag, odd_lag, got))
    elif (to_odd or to_even) and t < len(own):
        got = exchanged(after(own[t], *gate), lambda i: i >= 2 * t and (to_even if i % 2 else to_odd))
        other.append(got)
        new.append((even_lag, odd_lag, got))
    if memory % 2 == 0 and t == memory // 2 and devices - 2 >= memory - 1:
        got = upward(after(other[t - 1], *gate), lambda i: i % 2 == 0 and i + 2 >= memory - 1)
        new.append((memory - 1, None, got))
    return new


def shift_round(memory):
    if memory % 2:
        t = (memory - 1) // 2
    else:
        t = memory // 2 - 1 if lax.axis_size("tm") - 2 < memory - 1 else 0
    return t if t >= 2 else None


def next_in_chain(t, own, memory, gate):
    devices = lax.axis_size("tm")
    if t + 1 >= memory:
        return []
    got = lax.ppermute(after(own[t], *gate), "tm", [(i, i + 1) for i in range(devices - 1)])
    own.append(got)
    return [(t + 1, t + 1, got)]


def marker_kernel(value_ref, out_ref):
    out_ref[...] = jnp.zeros_like(out_ref)


def marker(value):
    zeros = pl.pallas_call(
        marker_kernel,
        out_shape=jax.ShapeDtypeStruct((8, 128), jnp.float32),
        in_specs=[pl.BlockSpec(memory_space=pl.ANY)],
        out_specs=pl.BlockSpec(memory_space=pltpu.VMEM),
        compiler_params=pltpu.CompilerParams(vmem_limit_bytes=VMEM_LIMIT),
        cost_estimate=pl.CostEstimate(flops=MARKER_COST, bytes_accessed=1024, transcendentals=0),
    )(value)
    return zeros[0, 0]


def bit_reversed(n):
    bits = n.bit_length() - 1
    return [sum(((p >> b) & 1) << (bits - 1 - b) for b in range(bits)) for p in range(n)]


def branch(memory, band, blocks, coef):
    orb = lax.axis_size("orb")
    lag_count = band.shape[2]
    paired = lax.axis_size("tm") % 2 == 0
    odd = lax.axis_index("tm") % 2 == 1
    power_of_two = orb & (orb - 1) == 0 and orb > 1
    order = jnp.array(bit_reversed(orb) if power_of_two else list(range(orb)), jnp.int32)
    columns = order ^ lax.axis_index("orb").astype(jnp.int32) if power_of_two else order
    count = len(blocks)
    own = [[block] for block in blocks]
    other = [[] for _ in blocks]
    arrived = [[[(0, 0, block)]] for block in blocks]
    totals = [None] * count

    def lag_of(even_lag, odd_lag):
        if even_lag == odd_lag:
            return even_lag
        none = lag_count
        return jnp.where(odd, none if odd_lag is None else odd_lag, none if even_lag is None else even_lag)

    def receive(t, q, gate):
        if paired:
            by_shift = t == shift_round(memory) and count > 2 and q >= (count + 1) // 2
            new = moves(t, own[q], other[q], memory, by_shift, gate)
        else:
            new = next_in_chain(t, own[q], memory, gate)
        if new:
            arrived[q].append(new)
        return bool(new)

    def multiply(r, q, first, tiles, total):
        new = arrived[q][r]
        lags = [lag_of(e, o) for e, o, _ in new]
        return products(band, coef, [b for _, _, b in new], lags, columns, total, first, tiles)

    gate = ()
    round_at = 0
    more = True
    while more:
        more = False
        for q in range(count):
            together = tuple(b for _, _, b in arrived[q][-1])
            more = receive(round_at, q, gate + together) or more
            if round_at + 1 < len(arrived[q]):
                totals[q] = multiply(round_at, q, 0, orb, totals[q])
                if round_at > 0 or q == count - 1:
                    gate = (totals[q],)
        round_at += 1

    parts = []
    sending = arriving = None
    for q in range(count):
        r = len(arrived[q]) - 1
        if not power_of_two:
            total = multiply(r, q, 0, orb, totals[q])
            parts.append(lax.psum_scatter(total, "orb", scatter_dimension=0, tiled=True)[0].T)
            continue
        if sending is not None:
            totals[q] = after(totals[q], sending)
        elif count > 1:
            totals[q] = after(totals[q], *gate)
        sent = multiply(r, q, orb // 2, orb // 2, totals[q])
        own_tiles = orb // 2 - orb // 4
        onward = multiply(r, q, own_tiles, orb // 4, totals[q]) if orb // 4 else None
        kept = multiply(r, q, 0, own_tiles, totals[q])
        stride = 1
        while True:
            sending = sent
            got = lax.ppermute(sent, "orb", [(i, i ^ stride) for i in range(orb)])
            if onward is None:
                break
            half = kept.shape[0]
            sent = onward + got[half:]
            kept = kept + got[:half]
            onward = kept[half // 2:] if half > 1 else None
            kept = kept[:half // 2] if half > 1 else kept
            stride *= 2
            if arriving is not None and stride == orb // 2:
                sent = sent + marker(arriving)
        arriving = got
        parts.append((kept[0] + got[0]).T)
    return jnp.concatenate(parts, axis=1)


def local(self_energy, history, memory, startup_cut, weight_index, weight_table):
    lag_count = self_energy.shape[2]
    row_total = self_energy.shape[4]
    table_size = weight_table.shape[0]
    lag_ids = jnp.arange(lag_count + 1, dtype=jnp.int32)[:, None]
    row_ids = jnp.arange(row_total, dtype=jnp.int32)[None, :]
    table_ids = jnp.arange(table_size, dtype=jnp.int32)[None, :]
    weights = jnp.sum(
        jnp.where(weight_index[0][:, None] == table_ids, weight_table[None, :], jnp.float32(0.0)),
        axis=1,
    )
    weights = jnp.concatenate([weights, jnp.zeros((1,), jnp.float32)])
    last_lag = memory[0] - 1
    kept_mask = (lag_ids < last_lag) | (lag_ids == last_lag) & (row_ids >= startup_cut[0])
    coef = jnp.where(kept_mask, weights[:, None], jnp.float32(0.0))[:, None, :]
    signs = jnp.array([1.0, -1.0], jnp.float32)[:, None, None]
    _, components, depth, orbitals = history.shape
    width = orbitals // CHUNKS
    blocks = [
        jnp.transpose(history[0, :, :, q * width:(q + 1) * width] * signs, (2, 0, 1)).reshape(width, components * depth)
        for q in range(CHUNKS)
    ]
    least = min(LEAST_MEMORY, lag_count)
    choices = [functools.partial(branch, kept) for kept in range(least, lag_count + 1)]
    collision = lax.switch(jnp.clip(memory[0] - least, 0, len(choices) - 1), choices, self_energy, blocks, coef)
    return collision[None]


def solution(mesh):
    in_specs = (
        P("tm", None, None, "orb", None),
        P("tm", None, "orb", None),
        P(),
        P("tm"),
        P("tm", None),
        P(),
    )
    out_specs = P("tm", "orb", None)
    return jax.shard_map(local, mesh=mesh, in_specs=in_specs, out_specs=out_specs, check_vma=False)
```

```python
import functools

import jax
import jax.numpy as jnp
from jax import lax
from jax.experimental import pallas as pl
from jax.experimental.pallas import tpu as pltpu
from jax.sharding import PartitionSpec as P

CHUNKS = 2
LEAST_MEMORY = 3
MARKER_COST = 60 * 10**9
STEP = 128
SPAN = 512
VMEM_LIMIT = 20 * 1024 * 1024


def split(value):
    high = value.astype(jnp.bfloat16)
    low = (value - high.astype(jnp.float32)).astype(jnp.bfloat16)
    return high, low


def product_kernel(count, has_total, first, scalars, *refs):
    band_refs = refs[:count]
    coef_refs = refs[count:2 * count]
    block_refs = refs[2 * count:3 * count]
    rest = refs[3 * count:]
    if has_total:
        total_ref, out_ref, left_ref, right_ref = rest
    else:
        out_ref, left_ref, right_ref = rest
    depth = block_refs[0].shape[1]

    width = block_refs[0].shape[0]
    band_step = STEP if band_refs[0].shape[3] % STEP == 0 else band_refs[0].shape[3]
    band_steps = band_refs[0].shape[3] // band_step
    block_step = STEP if width % STEP == 0 else width

    @pl.when(pl.program_id(0) == 0)
    def _():
        for q in range(count):

            @pl.loop(0, width // block_step)
            def _(step):
                at = pl.ds(pl.multiple_of(step * block_step, block_step), block_step)
                high, low = split(block_refs[q][at, :])
                for place, part in enumerate((high, low, high)):
                    left_ref[at, pl.ds((3 * q + place) * depth, depth)] = part

    for q in range(count):

        @pl.loop(0, depth // band_step)
        def _(step):
            inner = pl.multiple_of(lax.rem(step, band_steps) * band_step, band_step)
            high, low = split(band_refs[q][0, lax.div(step, band_steps), 0, pl.ds(inner, band_step), :] * coef_refs[q][0])
            for place, part in enumerate((high, high, low)):
                at = pl.multiple_of((3 * q + place) * depth + step * band_step, band_step)
                right_ref[pl.ds(at, band_step), :] = part

    tile = pl.program_id(0)
    across = SPAN if width % SPAN == 0 else width

    @pl.loop(0, width // across)
    def _(step):
        at = pl.ds(pl.multiple_of(step * across, across), across)
        term = jnp.dot(left_ref[at, :], right_ref[...], preferred_element_type=jnp.float32)
        out_ref[tile, at, :] = total_ref[first + tile, at, :] + term if has_total else term


def products(band, coef, blocks, lags, columns, total, first, tiles):
    count = len(blocks)
    _, components, lag_count, depth, row_total = band.shape
    orb = columns.shape[0]
    rows = row_total // orb
    width = blocks[0].shape[0]
    picked = jnp.stack([jnp.asarray(lag, jnp.int32) for lag in lags])
    scalars = jnp.concatenate([jnp.minimum(picked, lag_count - 1), picked, columns[first:first + tiles]])

    def band_map(q, i, s):
        return (0, 0, s[q], 0, s[2 * count + i])

    def coef_map(q, i, s):
        return (s[count + q], 0, s[2 * count + i])

    in_specs = [pl.BlockSpec((1, components, 1, depth, rows), functools.partial(band_map, q)) for q in range(count)]
    in_specs += [pl.BlockSpec((1, 1, rows), functools.partial(coef_map, q)) for q in range(count)]
    in_specs += [pl.BlockSpec(memory_space=pltpu.VMEM) for _ in range(count)]
    operands = [band] * count + [coef] * count + list(blocks)
    if total is not None:
        in_specs.append(pl.BlockSpec(memory_space=pltpu.VMEM))
        operands.append(total)
    in_place = total is not None and tiles == orb
    return pl.pallas_call(
        functools.partial(product_kernel, count, total is not None, first),
        out_shape=jax.ShapeDtypeStruct((tiles, width, rows), jnp.float32),
        grid_spec=pltpu.PrefetchScalarGridSpec(
            num_scalar_prefetch=1,
            grid=(tiles,),
            in_specs=in_specs,
            out_specs=pl.BlockSpec(memory_space=pltpu.VMEM),
            scratch_shapes=[
                pltpu.VMEM((width, 3 * count * components * depth), jnp.bfloat16),
                pltpu.VMEM((3 * count * components * depth, rows), jnp.bfloat16),
            ],
        ),
        input_output_aliases={3 * count + 1: 0} if in_place else {},
        compiler_params=pltpu.CompilerParams(vmem_limit_bytes=VMEM_LIMIT),
        cost_estimate=pl.CostEstimate(flops=1024, bytes_accessed=1024, transcendentals=0),
    )(scalars, *operands)


def upward(value, valid):
    devices = lax.axis_size("tm")
    return lax.ppermute(value, "tm", [(i, i + 2) for i in range(devices - 2) if valid(i)])


def exchanged(value, valid):
    devices = lax.axis_size("tm")
    return lax.ppermute(value, "tm", [(i, i ^ 1) for i in range(devices) if (i ^ 1) < devices and valid(i)])


def after(value, *earlier):
    return lax.optimization_barrier((value,) + earlier)[0]


def moves(t, own, other, memory, by_shift, gate):
    devices = lax.axis_size("tm")
    new = []
    to_odd = 2 * t + 1 < memory
    to_even = 1 <= t and 2 * t - 1 < memory
    even_lag = 2 * t - 1 if to_even else None
    odd_lag = 2 * t + 1 if to_odd else None
    if 2 * (t + 1) < memory:
        got = upward(after(own[t], *gate), lambda i: i >= 2 * t)
        own.append(got)
        new.append((2 * t + 2, 2 * t + 2, got))
    if by_shift:

        def useful(i):
            lag = odd_lag if i % 2 else even_lag
            return lag is not None and i + 2 - lag >= 0

        got = upward(after(other[t - 1], *gate), useful)
        other.append(got)
        new.append((even_lag, odd_lag, got))
    elif (to_odd or to_even) and t < len(own):
        got = exchanged(after(own[t], *gate), lambda i: i >= 2 * t and (to_even if i % 2 else to_odd))
        other.append(got)
        new.append((even_lag, odd_lag, got))
    if memory % 2 == 0 and t == memory // 2 and devices - 2 >= memory - 1:
        got = upward(after(other[t - 1], *gate), lambda i: i % 2 == 0 and i + 2 >= memory - 1)
        new.append((memory - 1, None, got))
    return new


def shift_round(memory):
    if memory % 2:
        t = (memory - 1) // 2
    else:
        t = memory // 2 - 1 if lax.axis_size("tm") - 2 < memory - 1 else 0
    return t if t >= 2 else None


def next_in_chain(t, own, memory, gate):
    devices = lax.axis_size("tm")
    if t + 1 >= memory:
        return []
    got = lax.ppermute(after(own[t], *gate), "tm", [(i, i + 1) for i in range(devices - 1)])
    own.append(got)
    return [(t + 1, t + 1, got)]


def marker_kernel(value_ref, out_ref):
    out_ref[...] = jnp.zeros_like(out_ref)


def marker(value):
    zeros = pl.pallas_call(
        marker_kernel,
        out_shape=jax.ShapeDtypeStruct((8, 128), jnp.float32),
        in_specs=[pl.BlockSpec(memory_space=pl.ANY)],
        out_specs=pl.BlockSpec(memory_space=pltpu.VMEM),
        compiler_params=pltpu.CompilerParams(vmem_limit_bytes=VMEM_LIMIT),
        cost_estimate=pl.CostEstimate(flops=MARKER_COST, bytes_accessed=1024, transcendentals=0),
    )(value)
    return zeros[0, 0]


def bit_reversed(n):
    bits = n.bit_length() - 1
    return [sum(((p >> b) & 1) << (bits - 1 - b) for b in range(bits)) for p in range(n)]


def branch(memory, band, blocks, coef):
    orb = lax.axis_size("orb")
    lag_count = band.shape[2]
    paired = lax.axis_size("tm") % 2 == 0
    odd = lax.axis_index("tm") % 2 == 1
    power_of_two = orb & (orb - 1) == 0 and orb > 1
    order = jnp.array(bit_reversed(orb) if power_of_two else list(range(orb)), jnp.int32)
    columns = order ^ lax.axis_index("orb").astype(jnp.int32) if power_of_two else order
    count = len(blocks)
    own = [[block] for block in blocks]
    other = [[] for _ in blocks]
    arrived = [[[(0, 0, block)]] for block in blocks]
    totals = [None] * count

    def lag_of(even_lag, odd_lag):
        if even_lag == odd_lag:
            return even_lag
        none = lag_count
        return jnp.where(odd, none if odd_lag is None else odd_lag, none if even_lag is None else even_lag)

    def receive(t, q, gate):
        if paired:
            by_shift = t == shift_round(memory) and count > 2 and q >= (count + 1) // 2
            new = moves(t, own[q], other[q], memory, by_shift, gate)
        else:
            new = next_in_chain(t, own[q], memory, gate)
        if new:
            arrived[q].append(new)
        return bool(new)

    def multiply(r, q, first, tiles, total):
        new = arrived[q][r]
        lags = [lag_of(e, o) for e, o, _ in new]
        return products(band, coef, [b for _, _, b in new], lags, columns, total, first, tiles)

    gate = ()
    round_at = 0
    more = True
    while more:
        more = False
        for q in range(count):
            together = tuple(b for _, _, b in arrived[q][-1])
            more = receive(round_at, q, gate + together) or more
            if round_at + 1 < len(arrived[q]):
                totals[q] = multiply(round_at, q, 0, orb, totals[q])
                if round_at > 0 or q == count - 1:
                    gate = (totals[q],)
        round_at += 1

    parts = []
    sending = arriving = None
    for q in range(count):
        r = len(arrived[q]) - 1
        if not power_of_two:
            total = multiply(r, q, 0, orb, totals[q])
            parts.append(lax.psum_scatter(total, "orb", scatter_dimension=0, tiled=True)[0].T)
            continue
        if sending is not None:
            totals[q] = after(totals[q], sending)
        elif count > 1:
            totals[q] = after(totals[q], *gate)
        sent = multiply(r, q, orb // 2, orb // 2, totals[q])
        own_tiles = orb // 2 - orb // 4
        onward = multiply(r, q, own_tiles, orb // 4, totals[q]) if orb // 4 else None
        kept = multiply(r, q, 0, own_tiles, totals[q])
        stride = 1
        while True:
            sending = sent
            got = lax.ppermute(sent, "orb", [(i, i ^ stride) for i in range(orb)])
            if onward is None:
                break
            half = kept.shape[0]
            sent = onward + got[half:]
            kept = kept + got[:half]
            onward = kept[half // 2:] if half > 1 else None
            kept = kept[:half // 2] if half > 1 else kept
            stride *= 2
            if arriving is not None and stride == orb // 2:
                sent = sent + marker(arriving)
        arriving = got
        parts.append((kept[0] + got[0]).T)
    return jnp.concatenate(parts, axis=1)


def local(self_energy, history, memory, startup_cut, weight_index, weight_table):
    lag_count = self_energy.shape[2]
    row_total = self_energy.shape[4]
    table_size = weight_table.shape[0]
    lag_ids = jnp.arange(lag_count + 1, dtype=jnp.int32)[:, None]
    row_ids = jnp.arange(row_total, dtype=jnp.int32)[None, :]
    table_ids = jnp.arange(table_size, dtype=jnp.int32)[None, :]
    weights = jnp.sum(
        jnp.where(weight_index[0][:, None] == table_ids, weight_table[None, :], jnp.float32(0.0)),
        axis=1,
    )
    weights = jnp.concatenate([weights, jnp.zeros((1,), jnp.float32)])
    last_lag = memory[0] - 1
    kept_mask = (lag_ids < last_lag) | (lag_ids == last_lag) & (row_ids >= startup_cut[0])
    coef = jnp.where(kept_mask, weights[:, None], jnp.float32(0.0))[:, None, :]
    signs = jnp.array([1.0, -1.0], jnp.float32)[:, None, None]
    _, components, depth, orbitals = history.shape
    width = orbitals // CHUNKS
    blocks = [
        jnp.transpose(history[0, :, :, q * width:(q + 1) * width] * signs, (2, 0, 1)).reshape(width, components * depth)
        for q in range(CHUNKS)
    ]
    least = min(LEAST_MEMORY, lag_count)
    choices = [functools.partial(branch, kept) for kept in range(least, lag_count + 1)]
    collision = lax.switch(jnp.clip(memory[0] - least, 0, len(choices) - 1), choices, self_energy, blocks, coef)
    return collision[None]


def solution(mesh):
    in_specs = (
        P("tm", None, None, "orb", None),
        P("tm", None, "orb", None),
        P(),
        P("tm"),
        P("tm", None),
        P(),
    )
    out_specs = P("tm", "orb", None)
    return jax.shard_map(local, mesh=mesh, in_specs=in_specs, out_specs=out_specs, check_vma=False)
```
